512 devices in a mesh: section: 8 (over x, core), peer: 64 (over y, z).
Axes of the slice: x: 4, y: 8, z: 8, core: 2. Of those that a mesh axis runs over, the one named last changes fastest.
Arguments:
- rows_in: bfloat16 [8, 8192, 5120], P('section', 'peer')
- returned: bfloat16 [8, 8192, 5120], P('section', 'peer'), may hold values from -6 to 6
- norm_gain: bfloat16 [8, 5120], P('section'), may hold values from 0.099609375 to 1.8984375
- adapter_down: bfloat16 [8, 5120, 16], P('section'), may hold values from -0.078125 to 0.078125
- adapter_up: bfloat16 [8, 16, 5120], P('section'), may hold values from -1.5 to 1.5
- wiring: int32 [8, 64], P('section', 'peer'), may hold values from 0 to 63, as said below
Outputs:
- forward_rows: bfloat16 [8, 8192, 5120], P('section', 'peer')
- grad_down: float32 [8, 5120, 16], P('section')
- grad_up: float32 [8, 16, 5120], P('section')
The draws below stay inside these ranges and needn't reach their ends.
Inputs may be any that keep to these rules, and one draw needn't show every extreme that they name: For each section s there is a mask m below 16 with wiring[s, p] = p XOR m for every peer p; each section's entries are a permutation of the peers.
All inputs are finite; a program needn't handle non-finite values.
Results may differ from the reference program's by a relative error of at most 0.0058.
Values may be sent and summed in bfloat16 or wider, within the bound.
A program may use at most 64 MiB of HBM per device.

```python
import math
import jax
import jax.numpy as jnp
from jax import lax

D = 5120
R = 16
ROWS = 128
BITS = 4
REACH = 16
SECTIONS = 8
TOTAL_ROWS = 8192
N_PEER = 64


def draw_rows_in(key, part):
    base_key, row_key, col_key = jax.random.split(key, 3)
    shape = (SECTIONS, TOTAL_ROWS, D)
    base = jax.random.normal(base_key, shape, jnp.float32)
    row_scale = jnp.exp(jax.random.uniform(row_key, (SECTIONS, TOTAL_ROWS, 1), jnp.float32, math.log(0.01), math.log(0.1)))
    col_scale = jnp.exp(jax.random.uniform(col_key, (1, 1, D), jnp.float32, math.log(0.5), math.log(2.0)))
    return jnp.clip(base * row_scale * col_scale, -24.0, 24.0).astype(jnp.bfloat16)


def draw_wiring(key, part):
    section_ids = jnp.arange(SECTIONS, dtype=jnp.int32)
    section_masks = jax.random.randint(key, (SECTIONS,), 0, REACH, dtype=jnp.int32)
    section_masks = jnp.bitwise_or(section_masks, jnp.left_shift(jnp.ones((SECTIONS,), jnp.int32), section_ids % BITS))
    peer_ids = jnp.arange(N_PEER, dtype=jnp.int32)
    return jnp.bitwise_xor(peer_ids[None, :], section_masks[:, None])


def block_levels(own_key, shape, cuts, low, top_value):
    gain, own = 1.0, jax.random.fold_in(own_key, 6)
    for position, parts in cuts:
        heights = jnp.exp(jax.random.uniform(jax.random.fold_in(own, position), (parts,), jnp.float32, low / len(cuts), top_value / len(cuts)))
        gain = gain * jnp.repeat(heights, shape[position] // parts).reshape([-1 if axis == position else 1 for axis in range(len(shape))])
    return gain


def bell_draw(stream_key, shape, scale, limit, cuts=(), held_as=jnp.bfloat16):
    loudness = block_levels(stream_key, shape, cuts, -0.22, 0.18) if cuts else 1.0
    drawn = jax.random.normal(stream_key, shape, jnp.float32) * scale * loudness
    return jnp.minimum(jnp.maximum(drawn, -limit), limit).astype(held_as)


def setup_inputs(seed: int = 0) -> dict:
    arg_keys = jax.random.split(jax.random.key(seed), 7)
    rows_in = draw_rows_in(jax.random.fold_in(arg_keys[6], 71), 0)
    returned = bell_draw(arg_keys[1], (SECTIONS, TOTAL_ROWS, D), 1.0, 6.0, ((0, 8), (1, 64)))
    norm_gain = jnp.clip(1.0 + 0.18 * jax.random.normal(arg_keys[2], (SECTIONS, D), jnp.float32), 0.099609375, 1.8984375).astype(jnp.bfloat16)
    adapter_down = bell_draw(arg_keys[3], (SECTIONS, D, R), D ** -0.5, 0.078125, ((0, 8),))
    adapter_up = bell_draw(arg_keys[4], (SECTIONS, R, D), R ** -0.5, 1.5, ((0, 8),))
    wiring = draw_wiring(jax.random.fold_in(arg_keys[6], 71), 0)
    return {"rows_in": rows_in, "returned": returned, "norm_gain": norm_gain, "adapter_down": adapter_down, "adapter_up": adapter_up, "wiring": wiring}


EPSILON = 1e-05

def section_pass(operands):
    inputs, upstream, gain_row, down_matrix, up_matrix = operands
    inputs_f = inputs.astype(jnp.float32)
    mean_square = lax.optimization_barrier(jnp.mean(inputs_f * inputs_f, axis=-1, keepdims=True))
    normed = (inputs_f * lax.rsqrt(mean_square + EPSILON) * gain_row.astype(jnp.float32)).astype(jnp.bfloat16)
    latent = jnp.einsum('prd,dk->prk', normed.astype(jnp.float32), down_matrix.astype(jnp.float32)).astype(jnp.bfloat16)
    outputs = (inputs_f + jnp.einsum('prk,kd->prd', latent.astype(jnp.float32), up_matrix.astype(jnp.float32))).astype(jnp.bfloat16)
    grad_up_sum = jnp.einsum('prk,prd->kd', latent.astype(jnp.float32), upstream.astype(jnp.float32))
    latent_grad = jnp.einsum('prd,kd->prk', upstream.astype(jnp.float32), up_matrix.astype(jnp.float32)).astype(jnp.bfloat16)
    grad_down_sum = jnp.einsum('prd,prk->dk', normed.astype(jnp.float32), latent_grad.astype(jnp.float32))
    return (outputs, grad_down_sum / N_PEER, grad_up_sum / N_PEER)

def reference(rows_in, returned, norm_gain, adapter_down, adapter_up, wiring):
    inputs = rows_in.reshape(SECTIONS, N_PEER, ROWS, D)
    gradient_rows = returned.reshape(SECTIONS, N_PEER, ROWS, D)
    next_section = ((jnp.arange(SECTIONS, dtype=jnp.int32) + 1) % SECTIONS)[:, None]
    upstream = gradient_rows[next_section, wiring]
    outputs, grad_down, grad_up = lax.map(section_pass, (inputs, upstream, norm_gain, adapter_down, adapter_up))
    moved = jnp.zeros_like(outputs).at[next_section, wiring].set(outputs)
    return (moved.reshape(SECTIONS, TOTAL_ROWS, D), grad_down, grad_up)
```

```python
import functools

import jax
import jax.numpy as jnp
from jax import lax
from jax.experimental import pallas as pl
from jax.experimental.pallas import tpu as pltpu
from jax.sharding import PartitionSpec as P

MESH = pl.DeviceIdType.MESH
BF, F32 = jnp.bfloat16, jnp.float32
EPSILON = 1e-05
D, R, ROWS = 5120, 16, 128
SECTIONS, NY, NZ = 8, 8, 8
G = 16
C = 4
CH = ROWS // C
W = D // NY
TILES = W // 128


def wait_bytes(ref, sem):
    pltpu.make_async_copy(ref, ref, sem).wait()


def kernel(
    wiring, rows_hbm, ret_hbm, gain, down_t, up,
    fwd_hbm, gdown, gup,
    rows, ret, norm, out,
    s0, s1, s2, s3, p0, p1, p2, p3, q0, q1, q2, q3,
    up_prev, lat_send, lat_recv, lg_send, lg_recv,
    y_send, y_recv, z_send, z_recv, zg, fu, fd,
    send, recv, local, bulk_send, one_recv, two_recv,
):
    S, Pc, Q = (s0, s1, s2, s3), (p0, p1, p2, p3), (q0, q1, q2, q3)
    sec, peer = lax.axis_index("section"), lax.axis_index("peer")
    nxt, prv = lax.rem(sec + 1, SECTIONS), lax.rem(sec + SECTIONS - 1, SECTIONS)
    y, z = lax.div(peer, NZ), lax.rem(peer, NZ)
    g = lax.rem(peer, G)
    base = peer - g

    def member(k):
        z2 = lax.rem(z + lax.rem(k, NZ), NZ)
        b = lax.rem(lax.rem(y, 2) + lax.div(k, NZ), 2)
        return b * NZ + z2

    def y_peer(k):
        y2 = lax.rem(y + k, NY)
        return y2, y2 * NZ + z

    def z_peer(k):
        z2 = lax.rem(z + k, NZ)
        return z2, y * NZ + z2

    def put(src, dst, s_sem, r_sem, s, p):
        pltpu.make_async_remote_copy(
            src_ref=src, dst_ref=dst, send_sem=s_sem, recv_sem=r_sem, device_id=(s, p), device_id_type=MESH
        ).start()

    def loop(lo, hi, body):
        lax.fori_loop(lo, hi, lambda k, _: (body(k), None)[1], None)

    rows_in = [
        pltpu.make_async_copy(rows_hbm.at[pl.ds(CH * c, CH)], rows.at[pl.ds(CH * c, CH)], local.at[c]) for c in range(C)
    ]
    ret_in = pltpu.make_async_copy(ret_hbm, ret, local.at[C])
    for copy in rows_in:
        copy.start()
    ret_in.start()

    barrier = pltpu.get_barrier_semaphore()

    def greet(s, p):
        pl.semaphore_signal(barrier, inc=1, device_id=(s, p), device_id_type=MESH)

    loop(1, G, lambda k: greet(sec, base + member(k)))
    loop(0, G, lambda k: greet(nxt, base + member(k)))
    loop(0, G, lambda k: greet(prv, base + member(k)))
    loop(1, NY, lambda k: greet(sec, y_peer(k)[1]))
    loop(0, NY, lambda k: greet(prv, y_peer(k)[1]))
    loop(0, NY, lambda k: greet(nxt, y_peer(k)[1]))

    gain_f = gain[...].astype(F32)

    def normalise(i):
        part = pl.ds(pl.multiple_of(i * 16, 16), 16)
        x = rows[part, :].astype(F32)
        mean_square = jnp.mean(x * x, axis=-1, keepdims=True)
        norm[part, :] = (x * lax.rsqrt(mean_square + EPSILON) * gain_f).astype(BF)

    def latent_of(lo, n):
        return lax.dot_general(
            down_t[...], norm[pl.ds(lo, n), :], (((1,), (1,)), ((), ())), preferred_element_type=F32
        ).astype(BF)

    def outputs_of(c, latent):
        def columns(j):
            part = pl.ds(pl.multiple_of(j * W, W), W)
            o = rows[pl.ds(CH * c, CH), part].astype(F32) + lax.dot_general(
                latent, up[:, part], (((0,), (0,)), ((), ())), preferred_element_type=F32
            )
            o = o.astype(BF)
            S[c][j] = o[:16]
            S[c][j + NY] = o[16:]

        loop(0, NY, columns)
        Pc[c][g] = S[c][g]

    def first_hop(c):
        def one(k):
            j = member(k)
            put(S[c].at[j], Pc[c].at[g], bulk_send.at[c], one_recv.at[c], sec, base + j)

        loop(1, G, one)

    rows_in[0].wait()
    loop(0, CH // 16, normalise)
    latent_0 = latent_of(0, CH)
    outputs_of(0, latent_0)
    pl.semaphore_wait(barrier, 15 + 2 * G + 7 + 2 * NY)
    put(up, up_prev, send.at[0], recv.at[0], nxt, peer)
    first_hop(0)

    for c in range(1, C):
        rows_in[c].wait()
    loop(CH // 16, ROWS // 16, normalise)
    latent_r = latent_of(CH, ROWS - CH)
    latent = jnp.concatenate([latent_0, latent_r], axis=1)
    mask = jnp.bitwise_and(jnp.bitwise_xor(wiring[0, 0], peer), G - 1)
    pick = jnp.bitwise_xor(g, mask)

    def send_latent(k):
        r = member(k)
        hit = jnp.full((R, ROWS), pick, jnp.int32) == jnp.full((R, ROWS), r, jnp.int32)
        lat_send[r] = jnp.where(hit, latent.astype(F32), 0.0).astype(BF)
        put(lat_send.at[r], lat_recv.at[g], send.at[1], recv.at[1], nxt, base + r)

    loop(0, G, send_latent)
    outputs_of(1, latent[:, CH : 2 * CH])
    first_hop(1)

    ret_in.wait()
    wait_bytes(up_prev, recv.at[0])
    lg_send[...] = lax.dot_general(
        up_prev[...], ret[...], (((1,), (1,)), ((), ())), preferred_element_type=F32
    ).astype(BF)
    loop(0, G, lambda k: put(lg_send, lg_recv.at[g], send.at[2], recv.at[2], prv, base + member(k)))
    for c in range(2, C):
        outputs_of(c, latent[:, CH * c : CH * (c + 1)])
        first_hop(c)

    wait_bytes(lat_recv, recv.at[1])
    latent_here = lat_recv[0].astype(F32)
    for r in range(1, G):
        latent_here += lat_recv[r].astype(F32)
    latent_here = latent_here.astype(BF)
    wait_bytes(lg_recv, recv.at[2])
    grad_here = lg_recv[pick]

    def terms(j):
        part = pl.ds(pl.multiple_of(j * W, W), W)
        y_send[j, :R] = jnp.dot(latent_here, ret[:, part], preferred_element_type=F32).astype(BF)
        y_send[j, R:] = jnp.dot(grad_here, norm[:, part], preferred_element_type=F32).astype(BF)

    loop(0, NY, terms)
    y_recv[y] = y_send[y]

    def send_terms(k):
        y2, p = y_peer(k)
        put(y_send.at[y2], y_recv.at[y], send.at[3], recv.at[3], sec, p)

    loop(1, NY, send_terms)

    def second_hop(c):
        wait_bytes(Pc[c].at[pl.ds(0, G - 1)], one_recv.at[c])
        row = pl.ds(pl.multiple_of(CH * c + 16 * lax.div(g, NY), 16), 16)
        column = pl.ds(pl.multiple_of(lax.rem(g, NY) * W, W), W)

        def one(k):
            r = member(k)
            Q[c][r] = Pc[c][jnp.bitwise_xor(r, mask)]
            put(Q[c].at[r], out.at[row, column], bulk_send.at[C + c], two_recv.at[c], nxt, base + r)

        loop(0, G, one)

    second_hop(0)

    wait_bytes(y_recv.at[pl.ds(0, NY - 1)], recv.at[3])
    for i in range(2):
        part = pl.ds(R * i, R)
        total = y_recv[0, part].astype(F32)
        for k in range(1, NY):
            total += y_recv[k, part].astype(F32)
        for t in range(TILES):
            z_send[TILES * i + t] = total[:, 128 * t : 128 * (t + 1)].astype(BF)
    for t in range(2 * TILES, 2 * NZ):
        z_send[t] = jnp.zeros((R, 128), BF)
    z_recv[z] = z_send[pl.ds(2 * z, 2)]

    def send_sums(k):
        z2, p = z_peer(k)
        put(z_send.at[pl.ds(2 * z2, 2)], z_recv.at[z], send.at[4], recv.at[4], sec, p)

    loop(1, NZ, send_sums)
    second_hop(1)

    wait_bytes(z_recv.at[pl.ds(0, NZ - 1)], recv.at[4])
    total = z_recv[0].astype(F32)
    for k in range(1, NZ):
        total += z_recv[k].astype(F32)
    zg[pl.ds(2 * z, 2)] = total.astype(BF)

    def send_totals(k):
        _, p = z_peer(k)
        mine = zg.at[pl.ds(2 * z, 2)]
        put(mine, mine, send.at[5], recv.at[5], sec, p)

    loop(1, NZ, send_totals)
    second_hop(2)

    wait_bytes(zg.at[pl.ds(0, 2 * (NZ - 1))], recv.at[5])
    fd[y] = zg[TILES : 2 * TILES]

    def share_up(k):
        put(zg.at[pl.ds(0, TILES)], fu.at[y], send.at[6], recv.at[6], prv, y_peer(k)[1])

    def share_down(k):
        put(zg.at[pl.ds(TILES, TILES)], fd.at[y], send.at[7], recv.at[7], sec, y_peer(k)[1])

    loop(0, NY, share_up)
    loop(1, NY, share_down)
    second_hop(3)

    wait_bytes(fu, recv.at[6])
    wait_bytes(fd.at[pl.ds(0, NY - 1)], recv.at[7])
    scale = 1.0 / (NY * NZ)
    for k in range(NY):
        for t in range(TILES):
            part = pl.ds(W * k + 128 * t, 128)
            gup[:, part] = fu[k, t].astype(F32) * scale
            gdown[:, part] = fd[k, t].astype(F32) * scale

    rows_out = []
    for c in range(C):
        part = pl.ds(CH * c, CH)
        wait_bytes(out.at[part], two_recv.at[c])
        rows_out.append(pltpu.make_async_copy(out.at[part], fwd_hbm.at[part], local.at[C + 1 + c]))
        rows_out[c].start()
    for c in range(C):
        wait_bytes(S[c].at[pl.ds(0, G - 1)], bulk_send.at[c])
        wait_bytes(Q[c], bulk_send.at[C + c])
    wait_bytes(up_prev, send.at[0])
    wait_bytes(lat_send, send.at[1])
    wait_bytes(lg_recv, send.at[2])
    wait_bytes(y_send.at[pl.ds(0, NY - 1)], send.at[3])
    wait_bytes(z_send.at[pl.ds(0, 2 * (NZ - 1))], send.at[4])
    wait_bytes(zg.at[pl.ds(0, 2 * (NZ - 1))], send.at[5])
    wait_bytes(fu, send.at[6])
    wait_bytes(fd.at[pl.ds(0, NY - 1)], send.at[7])
    for copy in rows_out:
        copy.wait()


def shards(rows_in, returned, norm_gain, adapter_down, adapter_up, wiring):
    whole = pl.BlockSpec(memory_space=pltpu.VMEM)
    far = pl.BlockSpec(memory_space=pl.ANY)
    block = pltpu.VMEM((ROWS, D), BF)
    pieces = pltpu.VMEM((G, 16, W), BF)
    tiles = pltpu.VMEM((G, R, 128), BF)
    dma = pltpu.SemaphoreType.DMA
    fwd, down_t, up_sum = pl.pallas_call(
        kernel,
        out_shape=(
            jax.ShapeDtypeStruct((ROWS, D), BF),
            jax.ShapeDtypeStruct((R, D), F32),
            jax.ShapeDtypeStruct((R, D), F32),
        ),
        in_specs=[pl.BlockSpec(memory_space=pltpu.SMEM), far, far, whole, whole, whole],
        out_specs=(far, whole, whole),
        scratch_shapes=[block] * 4
        + [pieces] * (3 * C)
        + [pltpu.VMEM((R, D), BF), tiles, tiles, pltpu.VMEM((R, 128), BF), tiles]
        + [pltpu.VMEM((NY, 2 * R, W), BF)] * 2
        + [pltpu.VMEM((2 * NZ, R, 128), BF), pltpu.VMEM((NZ, 2, R, 128), BF), pltpu.VMEM((2 * NZ, R, 128), BF)]
        + [pltpu.VMEM((NY, TILES, R, 128), BF)] * 2
        + [dma((8,)), dma((8,)), dma((2 * C + 1,)), dma((2 * C,)), dma((C,)), dma((C,))],
        compiler_params=pltpu.CompilerParams(collective_id=0, has_side_effects=True, vmem_limit_bytes=40 << 20),
        name="adapter_step",
    )(wiring, rows_in[0], returned[0], norm_gain, adapter_down[0].T, adapter_up[0])
    return fwd[None], down_t.T[None], up_sum[None]


def solution(mesh):
    in_specs = (
        P("section", "peer", None),
        P("section", "peer", None),
        P("section", None),
        P("section", None, None),
        P("section", None, None),
        P("section", "peer"),
    )
    out_specs = (P("section", "peer", None), P("section", None, None), P("section", None, None))
    return jax.shard_map(shards, mesh=mesh, in_specs=in_specs, out_specs=out_specs, check_vma=False)
```

```python
import functools

import jax
import jax.numpy as jnp
from jax import lax
from jax.experimental import pallas as pl
from jax.experimental.pallas import tpu as pltpu
from jax.sharding import PartitionSpec as P

MESH = pl.DeviceIdType.MESH
BF, F32 = jnp.bfloat16, jnp.float32
EPSILON = 1e-05
D, R, ROWS = 5120, 16, 128
SECTIONS, NY, NZ = 8, 8, 8
G = 16
C = 4
CH = ROWS // C
W = D // NY
TILES = W // 128
OWNERS = TILES
WINDOW = 16
ORDER = "c0 N U L a0 c1 G a1 c2 T a2 c3 b0 Y a3 b1 Z b2 d3 F e3 E o0 o1 o2 o3"


def wait_bytes(ref, sem):
    pltpu.make_async_copy(ref, ref, sem).wait()


def kernel(
    wiring, rows_hbm, ret_hbm, gain_hbm, down_hbm, up_hbm,
    out, gdown, gup,
    rows, ret, norm, gain, down_t, up,
    s0, s1, s2, s3, p0, p1, p2, p3, q0, q1, q2, q3,
    up_prev, lat_send, lat_recv, lg_send, lg_recv,
    y_send, y_recv, z_send, z_recv, zg, fu, fd,
    send, recv, local, bulk_send, one_recv, two_recv,
):
    S, Pc, Q = (s0, s1, s2, s3), (p0, p1, p2, p3), (q0, q1, q2, q3)
    sec, peer = lax.axis_index("section"), lax.axis_index("peer")
    nxt, prv = lax.rem(sec + 1, SECTIONS), lax.rem(sec + SECTIONS - 1, SECTIONS)
    y, z = lax.div(peer, NZ), lax.rem(peer, NZ)
    g = lax.rem(peer, G)
    base = peer - g

    def member(k):
        z2 = lax.rem(z + lax.rem(k, NZ), NZ)
        b = lax.rem(lax.rem(y, 2) + lax.div(k, NZ), 2)
        return b * NZ + z2

    def y_peer(k):
        y2 = lax.rem(y + k, NY)
        return y2, y2 * NZ + z

    def z_peer(k):
        z2 = lax.rem(z + k, NZ)
        return z2, y * NZ + z2

    def put(src, dst, s_sem, r_sem, s, p):
        pltpu.make_async_remote_copy(
            src_ref=src, dst_ref=dst, send_sem=s_sem, recv_sem=r_sem, device_id=(s, p), device_id_type=MESH
        ).start()

    def loop(lo, hi, body):
        lax.fori_loop(lo, hi, lambda k, _: (body(k), None)[1], None)

    def load(src, dst, i):
        copy = pltpu.make_async_copy(src, dst, local.at[i])
        copy.start()
        return copy

    chunk = [pl.ds(CH * c, CH) for c in range(C)]
    rows_in = [load(rows_hbm.at[chunk[0]], rows.at[chunk[0]], 0)]
    gain_in, down_in = load(gain_hbm, gain, C + 1), load(down_hbm, down_t, C + 2)
    up_in = load(up_hbm, up, C + 3)
    rows_in += [load(rows_hbm.at[chunk[c]], rows.at[chunk[c]], c) for c in range(1, C)]
    ret_in = load(ret_hbm, ret, C)

    barrier = pltpu.get_barrier_semaphore()

    def greet(s, p):
        pl.semaphore_signal(barrier, inc=1, device_id=(s, p), device_id_type=MESH)

    loop(1, G, lambda k: greet(sec, base + member(k)))
    loop(0, G, lambda k: greet(nxt, base + member(k)))
    loop(0, G, lambda k: greet(prv, base + member(k)))
    loop(1, NY, lambda k: greet(sec, y_peer(k)[1]))
    loop(0, NY, lambda k: greet(prv, y_peer(k)[1]))
    loop(0, NY, lambda k: greet(nxt, y_peer(k)[1]))

    mask = jnp.bitwise_and(jnp.bitwise_xor(wiring[0, 0], peer), G - 1)
    pick = jnp.bitwise_xor(g, mask)
    latents, sent = {}, []

    def normalise(i):
        part = pl.ds(pl.multiple_of(i * 16, 16), 16)
        x = rows[part, :].astype(F32)
        mean_square = jnp.mean(x * x, axis=-1, keepdims=True)
        norm[part, :] = (x * lax.rsqrt(mean_square + EPSILON) * gain[...].astype(F32)).astype(BF)

    def latent_of(lo, n):
        loop(lo // 16, (lo + n) // 16, normalise)
        return lax.dot_general(
            down_t[...], norm[pl.ds(lo, n), :], (((1,), (1,)), ((), ())), preferred_element_type=F32
        ).astype(BF)

    def bulk(lo, hi, one):
        first = len(sent) - lo
        sent.extend(range(lo, hi))
        free = min(max(lo, WINDOW - first), hi)
        slot = lambda k: bulk_send.at[lax.rem(first + k, WINDOW)]

        def later(k):
            wait_bytes(S[0].at[0], slot(k))
            one(k, slot(k))

        loop(lo, free, lambda k: one(k, slot(k)))
        loop(free, hi, later)

    def outputs_of(c):
        latent = latents[c]

        def columns(j):
            part = pl.ds(pl.multiple_of(j * W, W), W)
            o = rows[chunk[c], part].astype(F32) + lax.dot_general(
                latent, up[:, part], (((0,), (0,)), ((), ())), preferred_element_type=F32
            )
            o = o.astype(BF)
            S[c][j] = o[:16]
            S[c][j + NY] = o[16:]

        loop(0, NY, columns)
        Pc[c][g] = S[c][g]

    def all_here():
        pl.semaphore_wait(barrier, 15 + 2 * G + 7 + 2 * NY)
        put(up, up_prev, send.at[0], recv.at[0], nxt, peer)

    def first_hop(c):
        def one(k, sem):
            j = member(k)
            put(S[c].at[j], Pc[c].at[g], sem, one_recv.at[c], sec, base + j)

        bulk(1, G, one)

    def second_hop(c, lo=0, hi=G):
        if lo == 0:
            wait_bytes(Pc[c].at[pl.ds(0, G - 1)], one_recv.at[c])
        row = pl.ds(pl.multiple_of(CH * c + 16 * lax.div(g, NY), 16), 16)
        column = pl.ds(pl.multiple_of(lax.rem(g, NY) * W, W), W)

        def one(k, sem):
            r = member(k)
            Q[c][r] = Pc[c][jnp.bitwise_xor(r, mask)]
            put(Q[c].at[r], out.at[row, column], sem, two_recv.at[c], nxt, base + r)

        bulk(lo, hi, one)

    def second_hop_near(c):
        second_hop(c, 0, G // 2)

    def second_hop_far(c):
        second_hop(c, G // 2, G)

    def other_latents():
        for c in range(1, C):
            rows_in[c].wait()
        rest = latent_of(CH, ROWS - CH)
        for c in range(1, C):
            latents[c] = rest[:, CH * (c - 1) : CH * c]
        latents["all"] = jnp.concatenate([latents[0], rest], axis=1).astype(F32)

    def send_latents():
        latent = latents["all"]

        def one(k):
            r = member(k)
            hit = jnp.full((R, ROWS), pick, jnp.int32) == jnp.full((R, ROWS), r, jnp.int32)
            lat_send[r] = jnp.where(hit, latent, 0.0).astype(BF)
            put(lat_send.at[r], lat_recv.at[g], send.at[1], recv.at[1], nxt, base + r)

        loop(0, G, one)

    def send_latent_grads():
        ret_in.wait()
        wait_bytes(up_prev, recv.at[0])
        lg_send[...] = lax.dot_general(
            up_prev[...], ret[...], (((1,), (1,)), ((), ())), preferred_element_type=F32
        ).astype(BF)
        loop(0, G, lambda k: put(lg_send, lg_recv.at[g], send.at[2], recv.at[2], prv, base + member(k)))

    def send_terms():
        wait_bytes(lat_recv, recv.at[1])
        latent_here = lat_recv[0].astype(F32)
        for r in range(1, G):
            latent_here += lat_recv[r].astype(F32)
        latent_here = latent_here.astype(BF)
        wait_bytes(lg_recv, recv.at[2])
        grad_here = lg_recv[pick]

        def terms(j):
            part = pl.ds(pl.multiple_of(j * W, W), W)
            y_send[j, :R] = jnp.dot(latent_here, ret[:, part], preferred_element_type=F32).astype(BF)
            y_send[j, R:] = jnp.dot(grad_here, norm[:, part], preferred_element_type=F32).astype(BF)

        loop(0, NY, terms)
        y_recv[y] = y_send[y]

        def one(k):
            y2, p = y_peer(k)
            put(y_send.at[y2], y_recv.at[y], send.at[3], recv.at[3], sec, p)

        loop(1, NY, one)

    def send_y_sums():
        wait_bytes(y_recv.at[pl.ds(0, NY - 1)], recv.at[3])
        for i in range(2):
            part = pl.ds(R * i, R)
            total = y_recv[0, part].astype(F32)
            for k in range(1, NY):
                total += y_recv[k, part].astype(F32)
            for t in range(TILES):
                z_send[TILES * i + t] = total[:, 128 * t : 128 * (t + 1)].astype(BF)

        @pl.when(z < OWNERS)
        def _():
            z_recv[z] = z_send[pl.ds(2 * z, 2)]

        def one(k):
            z2, p = z_peer(k)

            @pl.when(z2 < OWNERS)
            def _():
                put(z_send.at[pl.ds(2 * z2, 2)], z_recv.at[z], send.at[4], recv.at[4], sec, p)

        loop(1, NZ, one)

    def send_z_sums():
        @pl.when(z < OWNERS)
        def _():
            wait_bytes(z_recv.at[pl.ds(0, NZ - 1)], recv.at[4])
            total = z_recv[0].astype(F32)
            for k in range(1, NZ):
                total += z_recv[k].astype(F32)
            zg[pl.ds(2 * z, 2)] = total.astype(BF)

            def one(k):
                _, p = z_peer(k)
                mine = zg.at[pl.ds(2 * z, 2)]
                put(mine, mine, send.at[5], recv.at[5], sec, p)

            loop(1, NZ, one)

    def wait_owners(sem):
        @pl.when(z < OWNERS)
        def _():
            wait_bytes(zg.at[pl.ds(0, 2 * (OWNERS - 1))], sem)

        @pl.when(z >= OWNERS)
        def _():
            wait_bytes(zg.at[pl.ds(0, 2 * OWNERS)], sem)

    def send_totals():
        wait_owners(recv.at[5])
        fd[y] = zg[TILES : 2 * TILES]

        def share_up(k):
            put(zg.at[pl.ds(0, TILES)], fu.at[y], send.at[6], recv.at[6], prv, y_peer(k)[1])

        def share_down(k):
            put(zg.at[pl.ds(TILES, TILES)], fd.at[y], send.at[7], recv.at[7], sec, y_peer(k)[1])

        loop(0, NY, share_up)
        loop(1, NY, share_down)

    def gradients_out():
        wait_bytes(fu, recv.at[6])
        wait_bytes(fd.at[pl.ds(0, NY - 1)], recv.at[7])
        scale = 1.0 / (NY * NZ)
        for k in range(NY):
            for t in range(TILES):
                part = pl.ds(W * k + 128 * t, 128)
                gup[:, part] = fu[k, t].astype(F32) * scale
                gdown[:, part] = fd[k, t].astype(F32) * scale

    def rows_there(c):
        wait_bytes(out.at[chunk[c]], two_recv.at[c])

    rows_in[0].wait()
    gain_in.wait()
    down_in.wait()
    latents[0] = latent_of(0, CH)
    up_in.wait()
    steps = {
        "U": all_here, "N": other_latents, "L": send_latents, "G": send_latent_grads, "T": send_terms,
        "Y": send_y_sums, "Z": send_z_sums, "F": send_totals, "E": gradients_out,
    }
    for step in ORDER.split():
        if step in steps:
            steps[step]()
        else:
            {"c": outputs_of, "a": first_hop, "b": second_hop, "d": second_hop_near, "e": second_hop_far, "o": rows_there}[step[0]](int(step[1]))
    wait_bytes(up_prev, send.at[0])
    wait_bytes(lat_send, send.at[1])
    wait_bytes(lg_recv, send.at[2])
    wait_bytes(y_send.at[pl.ds(0, NY - 1)], send.at[3])
    wait_owners(send.at[4])

    @pl.when(z < OWNERS)
    def _():
        wait_bytes(zg.at[pl.ds(0, 2 * (NZ - 1))], send.at[5])

    wait_bytes(fu, send.at[6])
    wait_bytes(fd.at[pl.ds(0, NY - 1)], send.at[7])
    loop(0, WINDOW, lambda k: wait_bytes(S[0].at[0], bulk_send.at[k]))


def copy_out(*refs):
    sems = refs[-1]
    copies = [pltpu.make_async_copy(refs[i], refs[3 + i], sems.at[i]) for i in range(3)]
    for copy in copies:
        copy.start()
    for copy in copies:
        copy.wait()


def shards(rows_in, returned, norm_gain, adapter_down, adapter_up, wiring):
    whole = pl.BlockSpec(memory_space=pltpu.VMEM)
    far = pl.BlockSpec(memory_space=pltpu.HBM)
    anywhere = pl.BlockSpec(memory_space=pl.ANY)
    block = pltpu.VMEM((ROWS, D), BF)
    pieces = pltpu.VMEM((G, 16, W), BF)
    tiles = pltpu.VMEM((G, R, 128), BF)
    dma = pltpu.SemaphoreType.DMA
    operands = rows_in[0], returned[0], norm_gain, adapter_down[0].T, adapter_up[0]
    results = pl.pallas_call(
        kernel,
        out_shape=(
            jax.ShapeDtypeStruct((ROWS, D), BF),
            jax.ShapeDtypeStruct((R, D), F32),
            jax.ShapeDtypeStruct((R, D), F32),
        ),
        in_specs=[pl.BlockSpec(memory_space=pltpu.SMEM), far, far, far, far, far],
        out_specs=(anywhere, whole, whole),
        scratch_shapes=[block] * 3
        + [pltpu.VMEM((1, D), BF), pltpu.VMEM((R, D), BF), pltpu.VMEM((R, D), BF)]
        + [pieces] * (3 * C)
        + [pltpu.VMEM((R, D), BF), tiles, tiles, pltpu.VMEM((R, 128), BF), tiles]
        + [pltpu.VMEM((NY, 2 * R, W), BF)] * 2
        + [pltpu.VMEM((2 * NZ, R, 128), BF), pltpu.VMEM((NZ, 2, R, 128), BF), pltpu.VMEM((2 * NZ, R, 128), BF)]
        + [pltpu.VMEM((NY, TILES, R, 128), BF)] * 2
        + [dma((8,)), dma((8,)), dma((C + 4,)), dma((WINDOW,)), dma((C,)), dma((C,))],
        compiler_params=pltpu.CompilerParams(collective_id=0, has_side_effects=True, vmem_limit_bytes=40 << 20),
        name="adapter_step",
    )(wiring, *(pltpu.with_memory_space_constraint(v, pltpu.HBM) for v in operands))
    fwd, down_sum, up_sum = pl.pallas_call(
        copy_out,
        out_shape=tuple(jax.ShapeDtypeStruct(v.shape, v.dtype) for v in results),
        in_specs=[anywhere] * 3,
        out_specs=(anywhere,) * 3,
        scratch_shapes=[dma((3,))],
        name="copy_out",
    )(*(pltpu.with_memory_space_constraint(v, pltpu.VMEM) for v in results))
    return fwd[None], down_sum.T[None], up_sum[None]


def solution(mesh):
    in_specs = (
        P("section", "peer", None),
        P("section", "peer", None),
        P("section", None),
        P("section", None, None),
        P("section", None, None),
        P("section", "peer"),
    )
    out_specs = (P("section", "peer", None), P("section", None, None), P("section", None, None))
    return jax.shard_map(shards, mesh=mesh, in_specs=in_specs, out_specs=out_specs, check_vma=False)
```

```python
import functools

import jax
import jax.numpy as jnp
from jax import lax
from jax.experimental import pallas as pl
from jax.experimental.pallas import tpu as pltpu
from jax.sharding import PartitionSpec as P

MESH = pl.DeviceIdType.MESH
BF, F32 = jnp.bfloat16, jnp.float32
EPSILON = 1e-05
D, R, ROWS = 5120, 16, 128
SECTIONS, NY, NZ = 8, 8, 8
G = 16
C = 4
CH = ROWS // C
W = D // NY
TILES = W // 128
OWNERS = TILES
WINDOW = 16
ORDER = (
    "c0", "N", "U", "X", "a0", "L", "c1", "G", "a1", "c2",
    "K", "c3", "a2", "T", "b0", "Y", "a3", "b1", "Z", "b2",
    "d3", "F", "e3", "E", "o0", "o1", "o2", "o3",
)


def wait_bytes(ref, sem):
    pltpu.make_async_copy(ref, ref, sem).wait()


def kernel(
    wiring, rows_hbm, ret_hbm, gain_hbm, down_hbm, up_hbm,
    out, gdown, gup,
    rows, ret, norm, gain, down_t, up,
    s0, s1, s2, s3, p0, p1, p2, p3, q0, q1, q2, q3,
    up_prev, lat_send, lat_recv, lg_send, lg_recv, lat_here, lat_there, lg_here, lg_there,
    y_send, y_recv, z_send, z_recv, zg, fu, fd,
    send, recv, local, bulk_send, one_recv, two_recv,
):
    S, Pc, Q = (s0, s1, s2, s3), (p0, p1, p2, p3), (q0, q1, q2, q3)
    sec, peer = lax.axis_index("section"), lax.axis_index("peer")
    nxt, prv = lax.rem(sec + 1, SECTIONS), lax.rem(sec + SECTIONS - 1, SECTIONS)
    y, z = lax.div(peer, NZ), lax.rem(peer, NZ)
    g = lax.rem(peer, G)
    base = peer - g

    def member(k):
        z2 = lax.rem(z + 3 * lax.rem(k, NZ), NZ)
        b = lax.rem(lax.rem(y, 2) + lax.div(k, NZ), 2)
        return b * NZ + z2

    def y_peer(k):
        y2 = lax.rem(y + k, NY)
        return y2, y2 * NZ + z

    def z_peer(k):
        z2 = lax.rem(z + k, NZ)
        return z2, y * NZ + z2

    def put(src, dst, s_sem, r_sem, s, p):
        pltpu.make_async_remote_copy(
            src_ref=src, dst_ref=dst, send_sem=s_sem, recv_sem=r_sem, device_id=(s, p), device_id_type=MESH
        ).start()

    def loop(lo, hi, body):
        lax.fori_loop(lo, hi, lambda k, _: (body(k), None)[1], None)

    def load(src, dst, i):
        copy = pltpu.make_async_copy(src, dst, local.at[i])
        copy.start()
        return copy

    chunk = [pl.ds(CH * c, CH) for c in range(C)]
    rows_in = [load(rows_hbm.at[chunk[0]], rows.at[chunk[0]], 0)]
    gain_in, down_in = load(gain_hbm, gain, C + 1), load(down_hbm, down_t, C + 2)
    up_in = load(up_hbm, up, C + 3)
    rows_in += [load(rows_hbm.at[chunk[c]], rows.at[chunk[c]], c) for c in range(1, C)]
    ret_in = load(ret_hbm, ret, C)

    barrier = pltpu.get_barrier_semaphore()

    def greet(s, p):
        pl.semaphore_signal(barrier, inc=1, device_id=(s, p), device_id_type=MESH)

    loop(1, G, lambda k: greet(sec, base + member(k)))
    loop(0, G, lambda k: greet(nxt, base + member(k)))
    loop(0, G, lambda k: greet(prv, base + member(k)))
    loop(1, NY, lambda k: greet(sec, y_peer(k)[1]))
    loop(0, NY, lambda k: greet(prv, y_peer(k)[1]))
    loop(0, NY, lambda k: greet(nxt, y_peer(k)[1]))

    latents, sent = {}, []
    pair = peer + NZ * (1 - 2 * lax.rem(y, 2))

    def normalise(i):
        part = pl.ds(pl.multiple_of(i * 16, 16), 16)
        x = rows[part, :].astype(F32)
        mean_square = jnp.mean(x * x, axis=-1, keepdims=True)
        norm[part, :] = (x * lax.rsqrt(mean_square + EPSILON) * gain[...].astype(F32)).astype(BF)

    def latent_of(lo, n):
        loop(lo // 16, (lo + n) // 16, normalise)
        return lax.dot_general(
            down_t[...], norm[pl.ds(lo, n), :], (((1,), (1,)), ((), ())), preferred_element_type=F32
        ).astype(BF)

    def bulk(lo, hi, one):
        first = len(sent) - lo
        sent.extend(range(lo, hi))
        free = min(max(lo, WINDOW - first), hi)
        slot = lambda k: bulk_send.at[lax.rem(first + k, WINDOW)]

        def later(k):
            wait_bytes(S[0].at[0], slot(k))
            one(k, slot(k))

        loop(lo, free, lambda k: one(k, slot(k)))
        loop(free, hi, later)

    def outputs_of(c):
        latent = latents[c]

        def columns(j):
            part = pl.ds(j * W, W)
            o = rows[chunk[c], part].astype(F32) + lax.dot_general(
                latent, up[:, part], (((0,), (0,)), ((), ())), preferred_element_type=F32
            )
            o = o.astype(BF)
            S[c][j] = o[:16]
            S[c][j + NY] = o[16:]

        for j in range(NY):
            columns(j)
        Pc[c][g] = S[c][g]

    def all_here():
        pl.semaphore_wait(barrier, 15 + 2 * G + 7 + 2 * NY)
        put(up, up_prev, send.at[0], recv.at[0], nxt, peer)

    def first_hop(c):
        def one(k, sem):
            j = member(k)
            put(S[c].at[j], Pc[c].at[g], sem, one_recv.at[c], sec, base + j)

        bulk(1, G, one)

    def second_hop(c, lo=0, hi=G):
        if lo == 0:
            wait_bytes(Pc[c].at[pl.ds(0, G - 1)], one_recv.at[c])
        row = pl.ds(pl.multiple_of(CH * c + 16 * lax.div(g, NY), 16), 16)
        column = pl.ds(pl.multiple_of(lax.rem(g, NY) * W, W), W)

        def one(k, sem):
            r = member(k)
            Q[c][r] = Pc[c][jnp.bitwise_xor(r, mask)]
            put(Q[c].at[r], out.at[row, column], sem, two_recv.at[c], nxt, base + r)

        bulk(lo, hi, one)

    def second_hop_near(c):
        second_hop(c, 0, G // 2)

    def second_hop_far(c):
        second_hop(c, G // 2, G)

    def other_latents():
        for c in range(1, C):
            rows_in[c].wait()
        rest = latent_of(CH, ROWS - CH)
        for c in range(1, C):
            latents[c] = rest[:, CH * (c - 1) : CH * c]
        latents["all"] = jnp.concatenate([latents[0], rest], axis=1).astype(F32)

    def of_pair(there, here):
        crossed = jnp.full((R, ROWS), mask_y, jnp.int32) == 1
        return jnp.where(crossed, there[...].astype(F32), here[...].astype(F32))

    def swap_latents():
        lat_here[...] = latents["all"].astype(BF)
        put(lat_here, lat_there, send.at[8], recv.at[8], sec, pair)

    def send_latents():
        wait_bytes(lat_there, recv.at[8])
        latent = of_pair(lat_there, lat_here)

        def one(k):
            z2, p = z_peer(3 * k)
            hit = jnp.full((R, ROWS), pick, jnp.int32) == jnp.full((R, ROWS), z2, jnp.int32)
            lat_send[z2] = jnp.where(hit, latent, 0.0).astype(BF)
            put(lat_send.at[z2], lat_recv.at[z], send.at[1], recv.at[1], nxt, p)

        loop(0, NZ, one)

    def send_latent_grads():
        ret_in.wait()
        wait_bytes(up_prev, recv.at[0])
        lg_send[...] = lax.dot_general(
            up_prev[...], ret[...], (((1,), (1,)), ((), ())), preferred_element_type=F32
        ).astype(BF)
        loop(0, NZ, lambda k: put(lg_send, lg_recv.at[z], send.at[2], recv.at[2], prv, z_peer(3 * k)[1]))

    def swap_latent_grads():
        wait_bytes(lg_recv, recv.at[2])
        lg_here[...] = lg_recv[pick]
        put(lg_here, lg_there, send.at[9], recv.at[9], sec, pair)

    def send_terms():
        wait_bytes(lat_recv, recv.at[1])
        latent_here = lat_recv[0].astype(F32)
        for r in range(1, NZ):
            latent_here += lat_recv[r].astype(F32)
        latent_here = latent_here.astype(BF)
        wait_bytes(lg_there, recv.at[9])
        grad_here = of_pair(lg_there, lg_here).astype(BF)

        def terms(j):
            part = pl.ds(pl.multiple_of(j * W, W), W)
            y_send[j, :R] = jnp.dot(latent_here, ret[:, part], preferred_element_type=F32).astype(BF)
            y_send[j, R:] = jnp.dot(grad_here, norm[:, part], preferred_element_type=F32).astype(BF)

        loop(0, NY, terms)
        y_recv[y] = y_send[y]

        def one(k):
            y2, p = y_peer(k)
            put(y_send.at[y2], y_recv.at[y], send.at[3], recv.at[3], sec, p)

        loop(1, NY, one)

    def send_y_sums():
        wait_bytes(y_recv.at[pl.ds(0, NY - 1)], recv.at[3])
        for i in range(2):
            part = pl.ds(R * i, R)
            total = y_recv[0, part].astype(F32)
            for k in range(1, NY):
                total += y_recv[k, part].astype(F32)
            for t in range(TILES):
                z_send[TILES * i + t] = total[:, 128 * t : 128 * (t + 1)].astype(BF)

        @pl.when(z < OWNERS)
        def _():
            z_recv[z] = z_send[pl.ds(2 * z, 2)]

        def one(k):
            z2, p = z_peer(k)

            @pl.when(z2 < OWNERS)
            def _():
                put(z_send.at[pl.ds(2 * z2, 2)], z_recv.at[z], send.at[4], recv.at[4], sec, p)

        loop(1, NZ, one)

    def send_z_sums():
        @pl.when(z < OWNERS)
        def _():
            wait_bytes(z_recv.at[pl.ds(0, NZ - 1)], recv.at[4])
            total = z_recv[0].astype(F32)
            for k in range(1, NZ):
                total += z_recv[k].astype(F32)
            zg[pl.ds(2 * z, 2)] = total.astype(BF)

            def one(k):
                _, p = z_peer(k)
                mine = zg.at[pl.ds(2 * z, 2)]
                put(mine, mine, send.at[5], recv.at[5], sec, p)

            loop(1, NZ, one)

    def wait_owners(sem):
        @pl.when(z < OWNERS)
        def _():
            wait_bytes(zg.at[pl.ds(0, 2 * (OWNERS - 1))], sem)

        @pl.when(z >= OWNERS)
        def _():
            wait_bytes(zg.at[pl.ds(0, 2 * OWNERS)], sem)

    def send_totals():
        wait_owners(recv.at[5])
        fd[y] = zg[TILES : 2 * TILES]

        def share_up(k):
            put(zg.at[pl.ds(0, TILES)], fu.at[y], send.at[6], recv.at[6], prv, y_peer(k)[1])

        def share_down(k):
            put(zg.at[pl.ds(TILES, TILES)], fd.at[y], send.at[7], recv.at[7], sec, y_peer(k)[1])

        loop(0, NY, share_up)
        loop(1, NY, share_down)

    def gradients_out():
        wait_bytes(fu, recv.at[6])
        wait_bytes(fd.at[pl.ds(0, NY - 1)], recv.at[7])
        scale = 1.0 / (NY * NZ)
        for k in range(NY):
            for t in range(TILES):
                part = pl.ds(W * k + 128 * t, 128)
                gup[:, part] = fu[k, t].astype(F32) * scale
                gdown[:, part] = fd[k, t].astype(F32) * scale

    def rows_there(c):
        wait_bytes(out.at[chunk[c]], two_recv.at[c])

    rows_in[0].wait()
    gain_in.wait()
    down_in.wait()
    latents[0] = latent_of(0, CH)
    up_in.wait()
    mask = jnp.bitwise_and(jnp.bitwise_xor(wiring[0, 0], peer), G - 1)
    mask_z, mask_y = lax.rem(mask, NZ), lax.div(mask, NZ)
    pick = jnp.bitwise_xor(z, mask_z)
    steps = {
        "U": all_here, "N": other_latents, "X": swap_latents, "L": send_latents, "K": swap_latent_grads, "G": send_latent_grads, "T": send_terms,
        "Y": send_y_sums, "Z": send_z_sums, "F": send_totals, "E": gradients_out,
    }
    for step in ORDER:
        if step in steps:
            steps[step]()
        else:
            {"c": outputs_of, "a": first_hop, "b": second_hop, "d": second_hop_near, "e": second_hop_far, "o": rows_there}[step[0]](int(step[1]))
    wait_bytes(up_prev, send.at[0])
    wait_bytes(lat_send, send.at[1])
    wait_bytes(lg_recv, send.at[2])
    wait_bytes(lat_there, send.at[8])
    wait_bytes(lg_there, send.at[9])
    wait_bytes(y_send.at[pl.ds(0, NY - 1)], send.at[3])
    wait_owners(send.at[4])

    @pl.when(z < OWNERS)
    def _():
        wait_bytes(zg.at[pl.ds(0, 2 * (NZ - 1))], send.at[5])

    wait_bytes(fu, send.at[6])
    wait_bytes(fd.at[pl.ds(0, NY - 1)], send.at[7])
    loop(0, WINDOW, lambda k: wait_bytes(S[0].at[0], bulk_send.at[k]))


def copy_out(*refs):
    sems = refs[-1]
    copies = [pltpu.make_async_copy(refs[i], refs[3 + i], sems.at[i]) for i in range(3)]
    for copy in copies:
        copy.start()
    for copy in copies:
        copy.wait()


def shards(rows_in, returned, norm_gain, adapter_down, adapter_up, wiring):
    whole = pl.BlockSpec(memory_space=pltpu.VMEM)
    far = pl.BlockSpec(memory_space=pltpu.HBM)
    anywhere = pl.BlockSpec(memory_space=pl.ANY)
    block = pltpu.VMEM((ROWS, D), BF)
    pieces = pltpu.VMEM((G, 16, W), BF)
    tiles, tile = pltpu.VMEM((NZ, R, 128), BF), pltpu.VMEM((R, 128), BF)
    dma = pltpu.SemaphoreType.DMA
    operands = rows_in[0], returned[0], norm_gain, adapter_down[0].T, adapter_up[0]
    results = pl.pallas_call(
        kernel,
        out_shape=(
            jax.ShapeDtypeStruct((ROWS, D), BF),
            jax.ShapeDtypeStruct((R, D), F32),
            jax.ShapeDtypeStruct((R, D), F32),
        ),
        in_specs=[pl.BlockSpec(memory_space=pltpu.SMEM)] + [far] * 5,
        out_specs=(anywhere, whole, whole),
        scratch_shapes=[block] * 3
        + [pltpu.VMEM((1, D), BF), pltpu.VMEM((R, D), BF), pltpu.VMEM((R, D), BF)]
        + [pieces] * (3 * C)
        + [pltpu.VMEM((R, D), BF), tiles, tiles, tile, tiles]
        + [tile] * 4
        + [pltpu.VMEM((NY, 2 * R, W), BF)] * 2
        + [pltpu.VMEM((2 * NZ, R, 128), BF), pltpu.VMEM((NZ, 2, R, 128), BF), pltpu.VMEM((2 * NZ, R, 128), BF)]
        + [pltpu.VMEM((NY, TILES, R, 128), BF)] * 2
        + [dma((10,)), dma((10,)), dma((C + 4,)), dma((WINDOW,)), dma((C,)), dma((C,))],
        compiler_params=pltpu.CompilerParams(collective_id=0, has_side_effects=True, vmem_limit_bytes=40 << 20),
        name="adapter_step",
    )(wiring, *(pltpu.with_memory_space_constraint(v, pltpu.HBM) for v in operands))
    fwd, down_sum, up_sum = pl.pallas_call(
        copy_out,
        out_shape=tuple(jax.ShapeDtypeStruct(v.shape, v.dtype) for v in results),
        in_specs=[anywhere] * 3,
        out_specs=(anywhere,) * 3,
        scratch_shapes=[dma((3,))],
        name="copy_out",
    )(*(pltpu.with_memory_space_constraint(v, pltpu.VMEM) for v in results))
    return fwd[None], down_sum.T[None], up_sum[None]


def solution(mesh):
    in_specs = (
        P("section", "peer", None),
        P("section", "peer", None),
        P("section", None),
        P("section", None, None),
        P("section", None, None),
        P("section", "peer"),
    )
    out_specs = (P("section", "peer", None), P("section", None, None), P("section", None, None))
    return jax.shard_map(shards, mesh=mesh, in_specs=in_specs, out_specs=out_specs, check_vma=False)
```

```python
import functools

import jax
import jax.numpy as jnp
from jax import lax
from jax.experimental import pallas as pl
from jax.experimental.pallas import tpu as pltpu
from jax.sharding import PartitionSpec as P

MESH = pl.DeviceIdType.MESH
BF, F32 = jnp.bfloat16, jnp.float32
EPSILON = 1e-05
D, R, ROWS = 5120, 16, 128
SECTIONS, NY, NZ = 8, 8, 8
G = 16
C = 4
CH = ROWS // C
W = D // NY
TILES = W // 128
OWNERS = TILES
WINDOW = 22
ORDER = (
    "c0", "N", "U", "X", "a0", "L", "c1", "G", "a1", "c2",
    "K", "c3", "a2", "T", "b0", "Y", "a3", "d1", "Z", "e1",
    "b2", "F", "b3", "E", "o0", "o1", "o2", "o3",
)


def wait_bytes(ref, sem):
    pltpu.make_async_copy(ref, ref, sem).wait()


def kernel(
    wiring, rows_hbm, ret_hbm, gain_hbm, down_hbm, up_hbm,
    out, gdown, gup,
    rows, ret, norm, gain, down_t, up,
    s0, s1, s2, s3, p0, p1, p2, p3, q0, q1, q2, q3,
    up_prev, lat_send, lat_recv, lg_send, lg_recv, lat_here, lat_there, lg_here, lg_there,
    y_send, y_recv, z_send, z_recv, zg, fu, fd,
    send, recv, local, bulk_send, one_recv, two_recv,
):
    S, Pc, Q = (s0, s1, s2, s3), (p0, p1, p2, p3), (q0, q1, q2, q3)
    sec, peer = lax.axis_index("section"), lax.axis_index("peer")
    nxt, prv = lax.rem(sec + 1, SECTIONS), lax.rem(sec + SECTIONS - 1, SECTIONS)
    y, z = lax.div(peer, NZ), lax.rem(peer, NZ)
    g = lax.rem(peer, G)
    base = peer - g
    own = lax.rem(3 * z, NZ)

    def member(k):
        z2 = lax.rem(z + 3 * lax.rem(k, NZ), NZ)
        b = lax.rem(lax.rem(y, 2) + lax.div(k, NZ), 2)
        return b * NZ + z2

    def y_peer(k):
        y2 = lax.rem(y + k, NY)
        return y2, y2 * NZ + z

    def z_peer(k):
        z2 = lax.rem(z + k, NZ)
        return z2, y * NZ + z2

    def put(src, dst, s_sem, r_sem, s, p):
        pltpu.make_async_remote_copy(
            src_ref=src, dst_ref=dst, send_sem=s_sem, recv_sem=r_sem, device_id=(s, p), device_id_type=MESH
        ).start()

    def loop(lo, hi, body):
        lax.fori_loop(lo, hi, lambda k, _: (body(k), None)[1], None)

    def load(src, dst, i):
        copy = pltpu.make_async_copy(src, dst, local.at[i])
        copy.start()
        return copy

    chunk = [pl.ds(CH * c, CH) for c in range(C)]
    rows_in = [load(rows_hbm.at[chunk[0]], rows.at[chunk[0]], 0)]
    gain_in, down_in = load(gain_hbm, gain, C + 1), load(down_hbm, down_t, C + 2)
    up_in = load(up_hbm, up, C + 3)
    rows_in += [load(rows_hbm.at[chunk[c]], rows.at[chunk[c]], c) for c in range(1, C)]
    ret_in = load(ret_hbm, ret, C)

    barrier = pltpu.get_barrier_semaphore()

    def greet(s, p):
        pl.semaphore_signal(barrier, inc=1, device_id=(s, p), device_id_type=MESH)

    loop(1, G, lambda k: greet(sec, base + member(k)))
    loop(0, G, lambda k: greet(nxt, base + member(k)))
    loop(0, G, lambda k: greet(prv, base + member(k)))
    loop(1, NY, lambda k: greet(sec, y_peer(k)[1]))
    loop(0, NY, lambda k: greet(prv, y_peer(k)[1]))
    loop(0, NY, lambda k: greet(nxt, y_peer(k)[1]))

    latents, sent = {}, []
    pair = peer + NZ * (1 - 2 * lax.rem(y, 2))

    def normalise(i):
        part = pl.ds(pl.multiple_of(i * 16, 16), 16)
        x = rows[part, :].astype(F32)
        mean_square = jnp.mean(x * x, axis=-1, keepdims=True)
        norm[part, :] = (x * lax.rsqrt(mean_square + EPSILON) * gain[...].astype(F32)).astype(BF)

    def latent_of(lo, n):
        loop(lo // 16, (lo + n) // 16, normalise)
        return lax.dot_general(
            down_t[...], norm[pl.ds(lo, n), :], (((1,), (1,)), ((), ())), preferred_element_type=F32
        ).astype(BF)

    def bulk(lo, hi, one):
        first = len(sent) - lo
        sent.extend(range(lo, hi))
        free = min(max(lo, WINDOW - first), hi)
        slot = lambda k: bulk_send.at[lax.rem(first + k, WINDOW)]

        def later(k):
            wait_bytes(S[0].at[0], slot(k))
            one(k, slot(k))

        loop(lo, free, lambda k: one(k, slot(k)))
        loop(free, hi, later)

    def outputs_of(c):
        latent = latents[c]

        def columns(j):
            part = pl.ds(j * W, W)
            o = rows[chunk[c], part].astype(F32) + lax.dot_general(
                latent, up[:, part], (((0,), (0,)), ((), ())), preferred_element_type=F32
            )
            o = o.astype(BF)
            S[c][j] = o[:16]
            S[c][j + NY] = o[16:]

        for j in range(NY):
            columns(j)
        Pc[c][g] = S[c][g]

    def all_here():
        pl.semaphore_wait(barrier, 15 + 2 * G + 7 + 2 * NY)
        put(up, up_prev, send.at[0], recv.at[0], nxt, peer)

    def first_hop(c):
        def one(k, sem):
            j = member(k)
            put(S[c].at[j], Pc[c].at[g], sem, one_recv.at[c], sec, base + j)

        bulk(1, G, one)

    def second_hop(c, lo=0, hi=G):
        if lo == 0:
            wait_bytes(Pc[c].at[pl.ds(0, G - 1)], one_recv.at[c])
        row = pl.ds(pl.multiple_of(CH * c + 16 * lax.div(g, NY), 16), 16)
        column = pl.ds(pl.multiple_of(lax.rem(g, NY) * W, W), W)

        def one(k, sem):
            r = member(k)
            Q[c][r] = Pc[c][jnp.bitwise_xor(r, mask)]
            put(Q[c].at[r], out.at[row, column], sem, two_recv.at[c], nxt, base + r)

        bulk(lo, hi, one)

    def second_hop_near(c):
        second_hop(c, 0, G // 2)

    def second_hop_far(c):
        second_hop(c, G // 2, G)

    def other_latents():
        for c in range(1, C):
            rows_in[c].wait()
        rest = latent_of(CH, ROWS - CH)
        for c in range(1, C):
            latents[c] = rest[:, CH * (c - 1) : CH * c]
        latents["all"] = jnp.concatenate([latents[0], rest], axis=1).astype(F32)

    def of_pair(there, here):
        crossed = jnp.full((R, ROWS), mask_y, jnp.int32) == 1
        return jnp.where(crossed, there[...].astype(F32), here[...].astype(F32))

    def swap_latents():
        lat_here[...] = latents["all"].astype(BF)
        put(lat_here, lat_there, send.at[8], recv.at[8], sec, pair)

    def send_latents():
        wait_bytes(lat_there, recv.at[8])
        latent = of_pair(lat_there, lat_here)

        def one(k):
            z2, p = z_peer(3 * k)
            hit = jnp.full((R, ROWS), pick, jnp.int32) == jnp.full((R, ROWS), z2, jnp.int32)
            lat_send[z2] = jnp.where(hit, latent, 0.0).astype(BF)
            put(lat_send.at[z2], lat_recv.at[z], send.at[1], recv.at[1], nxt, p)

        loop(0, NZ, one)

    def send_latent_grads():
        ret_in.wait()
        wait_bytes(up_prev, recv.at[0])
        lg_send[...] = lax.dot_general(
            up_prev[...], ret[...], (((1,), (1,)), ((), ())), preferred_element_type=F32
        ).astype(BF)
        loop(0, NZ, lambda k: put(lg_send, lg_recv.at[z], send.at[2], recv.at[2], prv, z_peer(3 * k)[1]))

    def swap_latent_grads():
        wait_bytes(lg_recv, recv.at[2])
        lg_here[...] = lg_recv[pick]
        put(lg_here, lg_there, send.at[9], recv.at[9], sec, pair)

    def send_terms():
        wait_bytes(lat_recv, recv.at[1])
        latent_here = lat_recv[0].astype(F32)
        for r in range(1, NZ):
            latent_here += lat_recv[r].astype(F32)
        latent_here = latent_here.astype(BF)
        wait_bytes(lg_there, recv.at[9])
        grad_here = of_pair(lg_there, lg_here).astype(BF)

        def terms(j):
            part = pl.ds(pl.multiple_of(j * W, W), W)
            y_send[j, :R] = jnp.dot(latent_here, ret[:, part], preferred_element_type=F32).astype(BF)
            y_send[j, R:] = jnp.dot(grad_here, norm[:, part], preferred_element_type=F32).astype(BF)

        loop(0, NY, terms)
        y_recv[y] = y_send[y]

        def one(k):
            y2, p = y_peer(k)
            put(y_send.at[y2], y_recv.at[y], send.at[3], recv.at[3], sec, p)

        loop(1, NY, one)

    def send_y_sums():
        wait_bytes(y_recv.at[pl.ds(0, NY - 1)], recv.at[3])
        for i in range(2):
            part = pl.ds(R * i, R)
            total = y_recv[0, part].astype(F32)
            for k in range(1, NY):
                total += y_recv[k, part].astype(F32)
            for t in range(TILES):
                z_send[TILES * i + t] = total[:, 128 * t : 128 * (t + 1)].astype(BF)

        @pl.when(own < OWNERS)
        def _():
            z_recv[z] = z_send[pl.ds(2 * own, 2)]

        def one(k):
            z2, p = z_peer(k)
            theirs = lax.rem(3 * z2, NZ)

            @pl.when(theirs < OWNERS)
            def _():
                put(z_send.at[pl.ds(2 * theirs, 2)], z_recv.at[z], send.at[4], recv.at[4], sec, p)

        loop(1, NZ, one)

    def send_z_sums():
        @pl.when(own < OWNERS)
        def _():
            wait_bytes(z_recv.at[pl.ds(0, NZ - 1)], recv.at[4])
            total = z_recv[0].astype(F32)
            for k in range(1, NZ):
                total += z_recv[k].astype(F32)
            zg[pl.ds(2 * own, 2)] = total.astype(BF)

            def one(k):
                _, p = z_peer(k)
                mine = zg.at[pl.ds(2 * own, 2)]
                put(mine, mine, send.at[5], recv.at[5], sec, p)

            loop(1, NZ, one)

    def wait_owners(sem):
        @pl.when(own < OWNERS)
        def _():
            wait_bytes(zg.at[pl.ds(0, 2 * (OWNERS - 1))], sem)

        @pl.when(own >= OWNERS)
        def _():
            wait_bytes(zg.at[pl.ds(0, 2 * OWNERS)], sem)

    def send_totals():
        wait_owners(recv.at[5])
        fd[y] = zg[TILES : 2 * TILES]

        def share_up(k):
            put(zg.at[pl.ds(0, TILES)], fu.at[y], send.at[6], recv.at[6], prv, y_peer(k)[1])

        def share_down(k):
            put(zg.at[pl.ds(TILES, TILES)], fd.at[y], send.at[7], recv.at[7], sec, y_peer(k)[1])

        loop(0, NY, share_up)
        loop(1, NY, share_down)

    def gradients_out():
        wait_bytes(fu, recv.at[6])
        wait_bytes(fd.at[pl.ds(0, NY - 1)], recv.at[7])
        scale = 1.0 / (NY * NZ)
        for k in range(NY):
            for t in range(TILES):
                part = pl.ds(W * k + 128 * t, 128)
                gup[:, part] = fu[k, t].astype(F32) * scale
                gdown[:, part] = fd[k, t].astype(F32) * scale

    def rows_there(c):
        wait_bytes(out.at[chunk[c]], two_recv.at[c])

    rows_in[0].wait()
    gain_in.wait()
    down_in.wait()
    latents[0] = latent_of(0, CH)
    up_in.wait()
    mask = jnp.bitwise_and(jnp.bitwise_xor(wiring[0, 0], peer), G - 1)
    mask_z, mask_y = lax.rem(mask, NZ), lax.div(mask, NZ)
    pick = jnp.bitwise_xor(z, mask_z)
    steps = {
        "U": all_here, "N": other_latents, "X": swap_latents, "L": send_latents, "K": swap_latent_grads, "G": send_latent_grads, "T": send_terms,
        "Y": send_y_sums, "Z": send_z_sums, "F": send_totals, "E": gradients_out,
    }
    for step in ORDER:
        if step in steps:
            steps[step]()
        else:
            {"c": outputs_of, "a": first_hop, "b": second_hop, "d": second_hop_near, "e": second_hop_far, "o": rows_there}[step[0]](int(step[1]))
    wait_bytes(up_prev, send.at[0])
    wait_bytes(lat_send, send.at[1])
    wait_bytes(lg_recv, send.at[2])
    wait_bytes(lat_there, send.at[8])
    wait_bytes(lg_there, send.at[9])
    wait_bytes(y_send.at[pl.ds(0, NY - 1)], send.at[3])
    wait_owners(send.at[4])

    @pl.when(own < OWNERS)
    def _():
        wait_bytes(zg.at[pl.ds(0, 2 * (NZ - 1))], send.at[5])

    wait_bytes(fu, send.at[6])
    wait_bytes(fd.at[pl.ds(0, NY - 1)], send.at[7])
    loop(0, WINDOW, lambda k: wait_bytes(S[0].at[0], bulk_send.at[k]))


def copy_out(*refs):
    sems = refs[-1]
    copies = [pltpu.make_async_copy(refs[i], refs[3 + i], sems.at[i]) for i in range(3)]
    for copy in copies:
        copy.start()
    for copy in copies:
        copy.wait()


def shards(rows_in, returned, norm_gain, adapter_down, adapter_up, wiring):
    whole = pl.BlockSpec(memory_space=pltpu.VMEM)
    far = pl.BlockSpec(memory_space=pltpu.HBM)
    anywhere = pl.BlockSpec(memory_space=pl.ANY)
    block = pltpu.VMEM((ROWS, D), BF)
    pieces = pltpu.VMEM((G, 16, W), BF)
    tiles, tile = pltpu.VMEM((NZ, R, 128), BF), pltpu.VMEM((R, 128), BF)
    dma = pltpu.SemaphoreType.DMA
    operands = rows_in[0], returned[0], norm_gain, adapter_down[0].T, adapter_up[0]
    results = pl.pallas_call(
        kernel,
        out_shape=(
            jax.ShapeDtypeStruct((ROWS, D), BF),
            jax.ShapeDtypeStruct((R, D), F32),
            jax.ShapeDtypeStruct((R, D), F32),
        ),
        in_specs=[pl.BlockSpec(memory_space=pltpu.SMEM)] + [far] * 5,
        out_specs=(anywhere, whole, whole),
        scratch_shapes=[block] * 3
        + [pltpu.VMEM((1, D), BF), pltpu.VMEM((R, D), BF), pltpu.VMEM((R, D), BF)]
        + [pieces] * (3 * C)
        + [pltpu.VMEM((R, D), BF), tiles, tiles, tile, tiles]
        + [tile] * 4
        + [pltpu.VMEM((NY, 2 * R, W), BF)] * 2
        + [pltpu.VMEM((2 * NZ, R, 128), BF), pltpu.VMEM((NZ, 2, R, 128), BF), pltpu.VMEM((2 * NZ, R, 128), BF)]
        + [pltpu.VMEM((NY, TILES, R, 128), BF)] * 2
        + [dma((10,)), dma((10,)), dma((C + 4,)), dma((WINDOW,)), dma((C,)), dma((C,))],
        compiler_params=pltpu.CompilerParams(collective_id=0, has_side_effects=True, vmem_limit_bytes=40 << 20),
        name="adapter_step",
    )(wiring, *(pltpu.with_memory_space_constraint(v, pltpu.HBM) for v in operands))
    fwd, down_sum, up_sum = pl.pallas_call(
        copy_out,
        out_shape=tuple(jax.ShapeDtypeStruct(v.shape, v.dtype) for v in results),
        in_specs=[anywhere] * 3,
        out_specs=(anywhere,) * 3,
        scratch_shapes=[dma((3,))],
        name="copy_out",
    )(*(pltpu.with_memory_space_constraint(v, pltpu.VMEM) for v in results))
    return fwd[None], down_sum.T[None], up_sum[None]


def solution(mesh):
    in_specs = (
        P("section", "peer", None),
        P("section", "peer", None),
        P("section", None),
        P("section", None, None),
        P("section", None, None),
        P("section", "peer"),
    )
    out_specs = (P("section", "peer", None), P("section", None, None), P("section", None, None))
    return jax.shard_map(shards, mesh=mesh, in_specs=in_specs, out_specs=out_specs, check_vma=False)
```

```python
import functools

import jax
import jax.numpy as jnp
from jax import lax
from jax.experimental import pallas as pl
from jax.experimental.pallas import tpu as pltpu
from jax.sharding import PartitionSpec as P

MESH = pl.DeviceIdType.MESH
BF, F32 = jnp.bfloat16, jnp.float32
EPSILON = 1e-05
D, R, ROWS = 5120, 16, 128
SECTIONS, NY, NZ = 8, 8, 8
G = 16
C = 4
CH = ROWS // C
W = D // NY
TILES = W // 128
OWNERS = TILES
WINDOW = 16
ORDER = (
    "c0", "N", "U", "X", "a0", "L", "c1", "G", "a1", "c2",
    "K", "c3", "a2", "T", "b0", "Y", "a3", "d1", "Z", "e1",
    "b2", "F", "b3", "E", "o0", "o1", "o2", "o3",
)


def wait_bytes(ref, sem):
    pltpu.make_async_copy(ref, ref, sem).wait()


def kernel(
    wiring, rows_hbm, ret_hbm, gain_hbm, down_hbm, up_hbm,
    out, gdown, gup,
    rows, ret, norm, gain, down_t, up,
    s0, s1, s2, s3, p0, p1, p2, p3, q0, q1, q2, q3,
    up_prev, lat_send, lat_recv, lg_send, lg_recv, lat_here, lat_there, lg_here, lg_there,
    y_send, y_recv, z_send, z_recv, zg, fu, fd,
    send, recv, local, bulk_send, one_recv, two_recv,
):
    S, Pc, Q = (s0, s1, s2, s3), (p0, p1, p2, p3), (q0, q1, q2, q3)
    sec, peer = lax.axis_index("section"), lax.axis_index("peer")
    nxt, prv = lax.rem(sec + 1, SECTIONS), lax.rem(sec + SECTIONS - 1, SECTIONS)
    y, z = lax.div(peer, NZ), lax.rem(peer, NZ)
    g = lax.rem(peer, G)
    base = peer - g

    def member(k):
        z2 = lax.rem(z + 3 * lax.rem(k, NZ), NZ)
        b = lax.rem(lax.rem(y, 2) + lax.div(k, NZ), 2)
        return b * NZ + z2

    def y_peer(k):
        y2 = lax.rem(y + k, NY)
        return y2, y2 * NZ + z

    def z_peer(k):
        z2 = lax.rem(z + k, NZ)
        return z2, y * NZ + z2

    def put(src, dst, s_sem, r_sem, s, p):
        pltpu.make_async_remote_copy(
            src_ref=src, dst_ref=dst, send_sem=s_sem, recv_sem=r_sem, device_id=(s, p), device_id_type=MESH
        ).start()

    def loop(lo, hi, body):
        lax.fori_loop(lo, hi, lambda k, _: (body(k), None)[1], None)

    def load(src, dst, i):
        copy = pltpu.make_async_copy(src, dst, local.at[i])
        copy.start()
        return copy

    chunk = [pl.ds(CH * c, CH) for c in range(C)]
    rows_in = [load(rows_hbm.at[chunk[0]], rows.at[chunk[0]], 0)]
    gain_in, down_in = load(gain_hbm, gain, C + 1), load(down_hbm, down_t, C + 2)
    up_in = load(up_hbm, up, C + 3)
    rows_in += [load(rows_hbm.at[chunk[c]], rows.at[chunk[c]], c) for c in range(1, C)]
    ret_in = load(ret_hbm, ret, C)

    barrier = pltpu.get_barrier_semaphore()

    def greet(s, p):
        pl.semaphore_signal(barrier, inc=1, device_id=(s, p), device_id_type=MESH)

    loop(1, G, lambda k: greet(sec, base + member(k)))
    loop(0, G, lambda k: greet(nxt, base + member(k)))
    loop(0, G, lambda k: greet(prv, base + member(k)))
    loop(1, NY, lambda k: greet(sec, y_peer(k)[1]))
    loop(0, NY, lambda k: greet(prv, y_peer(k)[1]))
    loop(0, NY, lambda k: greet(nxt, y_peer(k)[1]))

    latents, sent = {}, []
    pair = peer + NZ * (1 - 2 * lax.rem(y, 2))

    def normalise(i):
        part = pl.ds(pl.multiple_of(i * 16, 16), 16)
        x = rows[part, :].astype(F32)
        mean_square = jnp.mean(x * x, axis=-1, keepdims=True)
        norm[part, :] = (x * lax.rsqrt(mean_square + EPSILON) * gain[...].astype(F32)).astype(BF)

    def latent_of(lo, n):
        loop(lo // 16, (lo + n) // 16, normalise)
        return lax.dot_general(
            down_t[...], norm[pl.ds(lo, n), :], (((1,), (1,)), ((), ())), preferred_element_type=F32
        ).astype(BF)

    def bulk(lo, hi, one):
        first = len(sent) - lo
        sent.extend(range(lo, hi))
        free = min(max(lo, WINDOW - first), hi)
        slot = lambda k: bulk_send.at[lax.rem(first + k, WINDOW)]

        def later(k):
            wait_bytes(S[0].at[0], slot(k))
            one(k, slot(k))

        loop(lo, free, lambda k: one(k, slot(k)))
        loop(free, hi, later)

    def outputs_of(c):
        latent = latents[c]

        def columns(j):
            part = pl.ds(j * W, W)
            o = rows[chunk[c], part].astype(F32) + lax.dot_general(
                latent, up[:, part], (((0,), (0,)), ((), ())), preferred_element_type=F32
            )
            o = o.astype(BF)
            S[c][j] = o[:16]
            S[c][j + NY] = o[16:]

        for j in range(NY):
            columns(j)
        Pc[c][g] = S[c][g]

    def all_here():
        pl.semaphore_wait(barrier, 15 + 2 * G + 7 + 2 * NY)
        put(up, up_prev, send.at[0], recv.at[0], nxt, peer)

    def first_hop(c):
        def one(k, sem):
            j = member(k)
            put(S[c].at[j], Pc[c].at[g], sem, one_recv.at[c], sec, base + j)

        bulk(1, G, one)

    def second_hop(c, lo=0, hi=G):
        if lo == 0:
            wait_bytes(Pc[c].at[pl.ds(0, G - 1)], one_recv.at[c])
        row = pl.ds(pl.multiple_of(CH * c + 16 * lax.div(g, NY), 16), 16)
        column = pl.ds(pl.multiple_of(lax.rem(g, NY) * W, W), W)

        def one(k, sem):
            r = member(k)
            Q[c][r] = Pc[c][jnp.bitwise_xor(r, mask)]
            put(Q[c].at[r], out.at[row, column], sem, two_recv.at[c], nxt, base + r)

        bulk(lo, hi, one)

    def second_hop_near(c):
        second_hop(c, 0, G // 2)

    def second_hop_far(c):
        second_hop(c, G // 2, G)

    def other_latents():
        for c in range(1, C):
            rows_in[c].wait()
        rest = latent_of(CH, ROWS - CH)
        for c in range(1, C):
            latents[c] = rest[:, CH * (c - 1) : CH * c]
        latents["all"] = jnp.concatenate([latents[0], rest], axis=1).astype(F32)

    def of_pair(there, here):
        crossed = jnp.full((R, ROWS), mask_y, jnp.int32) == 1
        return jnp.where(crossed, there[...].astype(F32), here[...].astype(F32))

    def swap_latents():
        lat_here[...] = latents["all"].astype(BF)
        put(lat_here, lat_there, send.at[8], recv.at[8], sec, pair)

    def send_latents():
        wait_bytes(lat_there, recv.at[8])
        latent = of_pair(lat_there, lat_here)

        def one(k):
            z2, p = z_peer(3 * k)
            hit = jnp.full((R, ROWS), pick, jnp.int32) == jnp.full((R, ROWS), z2, jnp.int32)
            lat_send[z2] = jnp.where(hit, latent, 0.0).astype(BF)
            put(lat_send.at[z2], lat_recv.at[z], send.at[1], recv.at[1], nxt, p)

        loop(0, NZ, one)

    def send_latent_grads():
        ret_in.wait()
        wait_bytes(up_prev, recv.at[0])
        lg_send[...] = lax.dot_general(
            up_prev[...], ret[...], (((1,), (1,)), ((), ())), preferred_element_type=F32
        ).astype(BF)
        loop(0, NZ, lambda k: put(lg_send, lg_recv.at[z], send.at[2], recv.at[2], prv, z_peer(3 * k)[1]))

    def swap_latent_grads():
        wait_bytes(lg_recv, recv.at[2])
        lg_here[...] = lg_recv[pick]
        put(lg_here, lg_there, send.at[9], recv.at[9], sec, pair)

    def send_terms():
        wait_bytes(lat_recv, recv.at[1])
        latent_here = lat_recv[0].astype(F32)
        for r in range(1, NZ):
            latent_here += lat_recv[r].astype(F32)
        latent_here = latent_here.astype(BF)
        wait_bytes(lg_there, recv.at[9])
        grad_here = of_pair(lg_there, lg_here).astype(BF)

        def terms(j):
            part = pl.ds(pl.multiple_of(j * W, W), W)
            y_send[j, :R] = jnp.dot(latent_here, ret[:, part], preferred_element_type=F32).astype(BF)
            y_send[j, R:] = jnp.dot(grad_here, norm[:, part], preferred_element_type=F32).astype(BF)

        loop(0, NY, terms)
        y_recv[y] = y_send[y]

        def one(k):
            y2, p = y_peer(k)
            put(y_send.at[y2], y_recv.at[y], send.at[3], recv.at[3], sec, p)

        loop(1, NY, one)

    def send_y_sums():
        wait_bytes(y_recv.at[pl.ds(0, NY - 1)], recv.at[3])
        for i in range(2):
            part = pl.ds(R * i, R)
            total = y_recv[0, part].astype(F32)
            for k in range(1, NY):
                total += y_recv[k, part].astype(F32)
            for t in range(TILES):
                z_send[TILES * i + t] = total[:, 128 * t : 128 * (t + 1)].astype(BF)

        @pl.when(z < OWNERS)
        def _():
            z_recv[z] = z_send[pl.ds(2 * z, 2)]

        def one(k):
            z2, p = z_peer(k)

            @pl.when(z2 < OWNERS)
            def _():
                put(z_send.at[pl.ds(2 * z2, 2)], z_recv.at[z], send.at[4], recv.at[4], sec, p)

        loop(1, NZ, one)

    def send_z_sums():
        @pl.when(z < OWNERS)
        def _():
            wait_bytes(z_recv.at[pl.ds(0, NZ - 1)], recv.at[4])
            total = z_recv[0].astype(F32)
            for k in range(1, NZ):
                total += z_recv[k].astype(F32)
            zg[pl.ds(2 * z, 2)] = total.astype(BF)

            def one(k):
                _, p = z_peer(k)
                mine = zg.at[pl.ds(2 * z, 2)]
                put(mine, mine, send.at[5], recv.at[5], sec, p)

            loop(1, NZ, one)

    def wait_owners(sem):
        @pl.when(z < OWNERS)
        def _():
            wait_bytes(zg.at[pl.ds(0, 2 * (OWNERS - 1))], sem)

        @pl.when(z >= OWNERS)
        def _():
            wait_bytes(zg.at[pl.ds(0, 2 * OWNERS)], sem)

    def send_totals():
        wait_owners(recv.at[5])
        fd[y] = zg[TILES : 2 * TILES]

        def share_up(k):
            put(zg.at[pl.ds(0, TILES)], fu.at[y], send.at[6], recv.at[6], prv, y_peer(k)[1])

        def share_down(k):
            put(zg.at[pl.ds(TILES, TILES)], fd.at[y], send.at[7], recv.at[7], sec, y_peer(k)[1])

        loop(0, NY, share_up)
        loop(1, NY, share_down)

    def gradients_out():
        wait_bytes(fu, recv.at[6])
        wait_bytes(fd.at[pl.ds(0, NY - 1)], recv.at[7])
        scale = 1.0 / (NY * NZ)
        for k in range(NY):
            for t in range(TILES):
                part = pl.ds(W * k + 128 * t, 128)
                gup[:, part] = fu[k, t].astype(F32) * scale
                gdown[:, part] = fd[k, t].astype(F32) * scale

    def rows_there(c):
        wait_bytes(out.at[chunk[c]], two_recv.at[c])

    rows_in[0].wait()
    gain_in.wait()
    down_in.wait()
    latents[0] = latent_of(0, CH)
    up_in.wait()
    mask = jnp.bitwise_and(jnp.bitwise_xor(wiring[0, 0], peer), G - 1)
    mask_z, mask_y = lax.rem(mask, NZ), lax.div(mask, NZ)
    pick = jnp.bitwise_xor(z, mask_z)
    steps = {
        "U": all_here, "N": other_latents, "X": swap_latents, "L": send_latents, "K": swap_latent_grads, "G": send_latent_grads, "T": send_terms,
        "Y": send_y_sums, "Z": send_z_sums, "F": send_totals, "E": gradients_out,
    }
    for step in ORDER:
        if step in steps:
            steps[step]()
        else:
            {"c": outputs_of, "a": first_hop, "b": second_hop, "d": second_hop_near, "e": second_hop_far, "o": rows_there}[step[0]](int(step[1]))
    wait_bytes(up_prev, send.at[0])
    wait_bytes(lat_send, send.at[1])
    wait_bytes(lg_recv, send.at[2])
    wait_bytes(lat_there, send.at[8])
    wait_bytes(lg_there, send.at[9])
    wait_bytes(y_send.at[pl.ds(0, NY - 1)], send.at[3])
    wait_owners(send.at[4])

    @pl.when(z < OWNERS)
    def _():
        wait_bytes(zg.at[pl.ds(0, 2 * (NZ - 1))], send.at[5])

    wait_bytes(fu, send.at[6])
    wait_bytes(fd.at[pl.ds(0, NY - 1)], send.at[7])
    loop(0, WINDOW, lambda k: wait_bytes(S[0].at[0], bulk_send.at[k]))


def copy_out(*refs):
    sems = refs[-1]
    copies = [pltpu.make_async_copy(refs[i], refs[3 + i], sems.at[i]) for i in range(3)]
    for copy in copies:
        copy.start()
    for copy in copies:
        copy.wait()


def shards(rows_in, returned, norm_gain, adapter_down, adapter_up, wiring):
    whole = pl.BlockSpec(memory_space=pltpu.VMEM)
    far = pl.BlockSpec(memory_space=pltpu.HBM)
    anywhere = pl.BlockSpec(memory_space=pl.ANY)
    block = pltpu.VMEM((ROWS, D), BF)
    pieces = pltpu.VMEM((G, 16, W), BF)
    tiles, tile = pltpu.VMEM((NZ, R, 128), BF), pltpu.VMEM((R, 128), BF)
    dma = pltpu.SemaphoreType.DMA
    operands = rows_in[0], returned[0], norm_gain, adapter_down[0].T, adapter_up[0]
    results = pl.pallas_call(
        kernel,
        out_shape=(
            jax.ShapeDtypeStruct((ROWS, D), BF),
            jax.ShapeDtypeStruct((R, D), F32),
            jax.ShapeDtypeStruct((R, D), F32),
        ),
        in_specs=[pl.BlockSpec(memory_space=pltpu.SMEM)] + [far] * 5,
        out_specs=(anywhere, whole, whole),
        scratch_shapes=[block] * 3
        + [pltpu.VMEM((1, D), BF), pltpu.VMEM((R, D), BF), pltpu.VMEM((R, D), BF)]
        + [pieces] * (3 * C)
        + [pltpu.VMEM((R, D), BF), tiles, tiles, tile, tiles]
        + [tile] * 4
        + [pltpu.VMEM((NY, 2 * R, W), BF)] * 2
        + [pltpu.VMEM((2 * NZ, R, 128), BF), pltpu.VMEM((NZ, 2, R, 128), BF), pltpu.VMEM((2 * NZ, R, 128), BF)]
        + [pltpu.VMEM((NY, TILES, R, 128), BF)] * 2
        + [dma((10,)), dma((10,)), dma((C + 4,)), dma((WINDOW,)), dma((C,)), dma((C,))],
        compiler_params=pltpu.CompilerParams(collective_id=0, has_side_effects=True, vmem_limit_bytes=40 << 20),
        name="adapter_step",
    )(wiring, *(pltpu.with_memory_space_constraint(v, pltpu.HBM) for v in operands))
    fwd, down_sum, up_sum = pl.pallas_call(
        copy_out,
        out_shape=tuple(jax.ShapeDtypeStruct(v.shape, v.dtype) for v in results),
        in_specs=[anywhere] * 3,
        out_specs=(anywhere,) * 3,
        scratch_shapes=[dma((3,))],
        name="copy_out",
    )(*(pltpu.with_memory_space_constraint(v, pltpu.VMEM) for v in results))
    return fwd[None], down_sum.T[None], up_sum[None]


def solution(mesh):
    in_specs = (
        P("section", "peer", None),
        P("section", "peer", None),
        P("section", None),
        P("section", None, None),
        P("section", None, None),
        P("section", "peer"),
    )
    out_specs = (P("section", "peer", None), P("section", None, None), P("section", None, None))
    return jax.shard_map(shards, mesh=mesh, in_specs=in_specs, out_specs=out_specs, check_vma=False)
```

```python
import functools

import jax
import jax.numpy as jnp
from jax import lax
from jax.experimental import pallas as pl
from jax.experimental.pallas import tpu as pltpu
from jax.sharding import PartitionSpec as P

MESH = pl.DeviceIdType.MESH
BF, F32 = jnp.bfloat16, jnp.float32
EPSILON = 1e-05
D, R, ROWS = 5120, 16, 128
SECTIONS, NY, NZ = 8, 8, 8
G = 16
C = 4
CH = ROWS // C
W = D // NY
TILES = W // 128
OWNERS = TILES
WINDOW = 22
ORDER = (
    "c0", "N", "U", "X", "a0", "L", "c1", "G", "a1", "c2",
    "K", "c3", "a2", "T", "b0", "Y", "a3", "d1", "Z", "e1",
    "b2", "F", "b3", "E", "o0", "o1", "o2", "o3",
)


def wait_bytes(ref, sem):
    pltpu.make_async_copy(ref, ref, sem).wait()


def kernel(
    wiring, rows_hbm, ret_hbm, gain_hbm, down_hbm, up_hbm,
    out, gdown, gup,
    rows, ret, norm, gain, down_t, up,
    s0, s1, s2, s3, p0, p1, p2, p3, q0, q1, q2, q3,
    up_prev, lat_send, lat_recv, lg_send, lg_recv, lat_here, lat_there, lg_here, lg_there,
    y_send, y_recv, z_send, z_recv, zg, fu, fd,
    send, recv, local, bulk_send, one_recv, two_recv,
):
    S, Pc, Q = (s0, s1, s2, s3), (p0, p1, p2, p3), (q0, q1, q2, q3)
    sec, peer = lax.axis_index("section"), lax.axis_index("peer")
    nxt, prv = lax.rem(sec + 1, SECTIONS), lax.rem(sec + SECTIONS - 1, SECTIONS)
    y, z = lax.div(peer, NZ), lax.rem(peer, NZ)
    g = lax.rem(peer, G)
    base = peer - g

    def member(k):
        z2 = lax.rem(z + 3 * lax.rem(k, NZ), NZ)
        b = lax.rem(lax.rem(y, 2) + lax.div(k, NZ), 2)
        return b * NZ + z2

    def y_peer(k):
        y2 = lax.rem(y + k, NY)
        return y2, y2 * NZ + z

    def z_peer(k):
        z2 = lax.rem(z + k, NZ)
        return z2, y * NZ + z2

    def put(src, dst, s_sem, r_sem, s, p):
        pltpu.make_async_remote_copy(
            src_ref=src, dst_ref=dst, send_sem=s_sem, recv_sem=r_sem, device_id=(s, p), device_id_type=MESH
        ).start()

    def loop(lo, hi, body):
        lax.fori_loop(lo, hi, lambda k, _: (body(k), None)[1], None)

    def load(src, dst, i):
        copy = pltpu.make_async_copy(src, dst, local.at[i])
        copy.start()
        return copy

    chunk = [pl.ds(CH * c, CH) for c in range(C)]
    rows_in = [load(rows_hbm.at[chunk[0]], rows.at[chunk[0]], 0)]
    gain_in, down_in = load(gain_hbm, gain, C + 1), load(down_hbm, down_t, C + 2)
    up_in = load(up_hbm, up, C + 3)
    rows_in += [load(rows_hbm.at[chunk[c]], rows.at[chunk[c]], c) for c in range(1, C)]
    ret_in = load(ret_hbm, ret, C)

    barrier = pltpu.get_barrier_semaphore()

    def greet(s, p):
        pl.semaphore_signal(barrier, inc=1, device_id=(s, p), device_id_type=MESH)

    loop(1, G, lambda k: greet(sec, base + member(k)))
    loop(0, G, lambda k: greet(nxt, base + member(k)))
    loop(0, G, lambda k: greet(prv, base + member(k)))
    loop(1, NY, lambda k: greet(sec, y_peer(k)[1]))
    loop(0, NY, lambda k: greet(prv, y_peer(k)[1]))
    loop(0, NY, lambda k: greet(nxt, y_peer(k)[1]))

    latents, sent = {}, []
    pair = peer + NZ * (1 - 2 * lax.rem(y, 2))

    def normalise(i):
        part = pl.ds(pl.multiple_of(i * 16, 16), 16)
        x = rows[part, :].astype(F32)
        mean_square = jnp.mean(x * x, axis=-1, keepdims=True)
        norm[part, :] = (x * lax.rsqrt(mean_square + EPSILON) * gain[...].astype(F32)).astype(BF)

    def latent_of(lo, n):
        loop(lo // 16, (lo + n) // 16, normalise)
        return lax.dot_general(
            down_t[...], norm[pl.ds(lo, n), :], (((1,), (1,)), ((), ())), preferred_element_type=F32
        ).astype(BF)

    def bulk(lo, hi, one):
        first = len(sent) - lo
        sent.extend(range(lo, hi))
        free = min(max(lo, WINDOW - first), hi)
        slot = lambda k: bulk_send.at[lax.rem(first + k, WINDOW)]

        def later(k):
            wait_bytes(S[0].at[0], slot(k))
            one(k, slot(k))

        loop(lo, free, lambda k: one(k, slot(k)))
        loop(free, hi, later)

    def outputs_of(c):
        latent = latents[c]

        def columns(j):
            part = pl.ds(j * W, W)
            o = rows[chunk[c], part].astype(F32) + lax.dot_general(
                latent, up[:, part], (((0,), (0,)), ((), ())), preferred_element_type=F32
            )
            o = o.astype(BF)
            S[c][j] = o[:16]
            S[c][j + NY] = o[16:]

        for j in range(NY):
            columns(j)
        Pc[c][g] = S[c][g]

    def all_here():
        pl.semaphore_wait(barrier, 15 + 2 * G + 7 + 2 * NY)
        put(up, up_prev, send.at[0], recv.at[0], nxt, peer)

    def first_hop(c):
        def one(k, sem):
            j = member(k)
            put(S[c].at[j], Pc[c].at[g], sem, one_recv.at[c], sec, base + j)

        bulk(1, G, one)

    def second_hop(c, lo=0, hi=G):
        if lo == 0:
            wait_bytes(Pc[c].at[pl.ds(0, G - 1)], one_recv.at[c])
        row = pl.ds(pl.multiple_of(CH * c + 16 * lax.div(g, NY), 16), 16)
        column = pl.ds(pl.multiple_of(lax.rem(g, NY) * W, W), W)

        def one(k, sem):
            r = member(k)
            Q[c][r] = Pc[c][jnp.bitwise_xor(r, mask)]
            put(Q[c].at[r], out.at[row, column], sem, two_recv.at[c], nxt, base + r)

        bulk(lo, hi, one)

    def second_hop_near(c):
        second_hop(c, 0, G // 2)

    def second_hop_far(c):
        second_hop(c, G // 2, G)

    def other_latents():
        for c in range(1, C):
            rows_in[c].wait()
        rest = latent_of(CH, ROWS - CH)
        for c in range(1, C):
            latents[c] = rest[:, CH * (c - 1) : CH * c]
        latents["all"] = jnp.concatenate([latents[0], rest], axis=1).astype(F32)

    def of_pair(there, here):
        crossed = jnp.full((R, ROWS), mask_y, jnp.int32) == 1
        return jnp.where(crossed, there[...].astype(F32), here[...].astype(F32))

    def swap_latents():
        lat_here[...] = latents["all"].astype(BF)
        put(lat_here, lat_there, send.at[8], recv.at[8], sec, pair)

    def send_latents():
        wait_bytes(lat_there, recv.at[8])
        latent = of_pair(lat_there, lat_here)

        def one(k):
            z2, p = z_peer(3 * k)
            hit = jnp.full((R, ROWS), pick, jnp.int32) == jnp.full((R, ROWS), z2, jnp.int32)
            lat_send[z2] = jnp.where(hit, latent, 0.0).astype(BF)
            put(lat_send.at[z2], lat_recv.at[z], send.at[1], recv.at[1], nxt, p)

        loop(0, NZ, one)

    def send_latent_grads():
        ret_in.wait()
        wait_bytes(up_prev, recv.at[0])
        lg_send[...] = lax.dot_general(
            up_prev[...], ret[...], (((1,), (1,)), ((), ())), preferred_element_type=F32
        ).astype(BF)
        loop(0, NZ, lambda k: put(lg_send, lg_recv.at[z], send.at[2], recv.at[2], prv, z_peer(3 * k)[1]))

    def swap_latent_grads():
        wait_bytes(lg_recv, recv.at[2])
        lg_here[...] = lg_recv[pick]
        put(lg_here, lg_there, send.at[9], recv.at[9], sec, pair)

    def send_terms():
        wait_bytes(lat_recv, recv.at[1])
        latent_here = lat_recv[0].astype(F32)
        for r in range(1, NZ):
            latent_here += lat_recv[r].astype(F32)
        latent_here = latent_here.astype(BF)
        wait_bytes(lg_there, recv.at[9])
        grad_here = of_pair(lg_there, lg_here).astype(BF)

        def terms(j):
            part = pl.ds(pl.multiple_of(j * W, W), W)
            y_send[j, :R] = jnp.dot(latent_here, ret[:, part], preferred_element_type=F32).astype(BF)
            y_send[j, R:] = jnp.dot(grad_here, norm[:, part], preferred_element_type=F32).astype(BF)

        loop(0, NY, terms)
        y_recv[y] = y_send[y]

        def one(k):
            y2, p = y_peer(k)
            put(y_send.at[y2], y_recv.at[y], send.at[3], recv.at[3], sec, p)

        loop(1, NY, one)

    def send_y_sums():
        wait_bytes(y_recv.at[pl.ds(0, NY - 1)], recv.at[3])
        for i in range(2):
            part = pl.ds(R * i, R)
            total = y_recv[0, part].astype(F32)
            for k in range(1, NY):
                total += y_recv[k, part].astype(F32)
            for t in range(TILES):
                z_send[TILES * i + t] = total[:, 128 * t : 128 * (t + 1)].astype(BF)

        @pl.when(z < OWNERS)
        def _():
            z_recv[z] = z_send[pl.ds(2 * z, 2)]

        def one(k):
            z2, p = z_peer(k)

            @pl.when(z2 < OWNERS)
            def _():
                put(z_send.at[pl.ds(2 * z2, 2)], z_recv.at[z], send.at[4], recv.at[4], sec, p)

        loop(1, NZ, one)

    def send_z_sums():
        @pl.when(z < OWNERS)
        def _():
            wait_bytes(z_recv.at[pl.ds(0, NZ - 1)], recv.at[4])
            total = z_recv[0].astype(F32)
            for k in range(1, NZ):
                total += z_recv[k].astype(F32)
            zg[pl.ds(2 * z, 2)] = total.astype(BF)

            def one(k):
                _, p = z_peer(k)
                mine = zg.at[pl.ds(2 * z, 2)]
                put(mine, mine, send.at[5], recv.at[5], sec, p)

            loop(1, NZ, one)

    def wait_owners(sem):
        @pl.when(z < OWNERS)
        def _():
            wait_bytes(zg.at[pl.ds(0, 2 * (OWNERS - 1))], sem)

        @pl.when(z >= OWNERS)
        def _():
            wait_bytes(zg.at[pl.ds(0, 2 * OWNERS)], sem)

    def send_totals():
        wait_owners(recv.at[5])
        fd[y] = zg[TILES : 2 * TILES]

        def share_up(k):
            put(zg.at[pl.ds(0, TILES)], fu.at[y], send.at[6], recv.at[6], prv, y_peer(k)[1])

        def share_down(k):
            put(zg.at[pl.ds(TILES, TILES)], fd.at[y], send.at[7], recv.at[7], sec, y_peer(k)[1])

        loop(0, NY, share_up)
        loop(1, NY, share_down)

    def gradients_out():
        wait_bytes(fu, recv.at[6])
        wait_bytes(fd.at[pl.ds(0, NY - 1)], recv.at[7])
        scale = 1.0 / (NY * NZ)
        for k in range(NY):
            for t in range(TILES):
                part = pl.ds(W * k + 128 * t, 128)
                gup[:, part] = fu[k, t].astype(F32) * scale
                gdown[:, part] = fd[k, t].astype(F32) * scale

    def rows_there(c):
        wait_bytes(out.at[chunk[c]], two_recv.at[c])

    rows_in[0].wait()
    gain_in.wait()
    down_in.wait()
    latents[0] = latent_of(0, CH)
    up_in.wait()
    mask = jnp.bitwise_and(jnp.bitwise_xor(wiring[0, 0], peer), G - 1)
    mask_z, mask_y = lax.rem(mask, NZ), lax.div(mask, NZ)
    pick = jnp.bitwise_xor(z, mask_z)
    steps = {
        "U": all_here, "N": other_latents, "X": swap_latents, "L": send_latents, "K": swap_latent_grads, "G": send_latent_grads, "T": send_terms,
        "Y": send_y_sums, "Z": send_z_sums, "F": send_totals, "E": gradients_out,
    }
    for step in ORDER:
        if step in steps:
            steps[step]()
        else:
            {"c": outputs_of, "a": first_hop, "b": second_hop, "d": second_hop_near, "e": second_hop_far, "o": rows_there}[step[0]](int(step[1]))
    wait_bytes(up_prev, send.at[0])
    wait_bytes(lat_send, send.at[1])
    wait_bytes(lg_recv, send.at[2])
    wait_bytes(lat_there, send.at[8])
    wait_bytes(lg_there, send.at[9])
    wait_bytes(y_send.at[pl.ds(0, NY - 1)], send.at[3])
    wait_owners(send.at[4])

    @pl.when(z < OWNERS)
    def _():
        wait_bytes(zg.at[pl.ds(0, 2 * (NZ - 1))], send.at[5])

    wait_bytes(fu, send.at[6])
    wait_bytes(fd.at[pl.ds(0, NY - 1)], send.at[7])
    loop(0, WINDOW, lambda k: wait_bytes(S[0].at[0], bulk_send.at[k]))


def copy_out(*refs):
    sems = refs[-1]
    copies = [pltpu.make_async_copy(refs[i], refs[3 + i], sems.at[i]) for i in range(3)]
    for copy in copies:
        copy.start()
    for copy in copies:
        copy.wait()


def shards(rows_in, returned, norm_gain, adapter_down, adapter_up, wiring):
    whole = pl.BlockSpec(memory_space=pltpu.VMEM)
    far = pl.BlockSpec(memory_space=pltpu.HBM)
    anywhere = pl.BlockSpec(memory_space=pl.ANY)
    block = pltpu.VMEM((ROWS, D), BF)
    pieces = pltpu.VMEM((G, 16, W), BF)
    tiles, tile = pltpu.VMEM((NZ, R, 128), BF), pltpu.VMEM((R, 128), BF)
    dma = pltpu.SemaphoreType.DMA
    operands = rows_in[0], returned[0], norm_gain, adapter_down[0].T, adapter_up[0]
    results = pl.pallas_call(
        kernel,
        out_shape=(
            jax.ShapeDtypeStruct((ROWS, D), BF),
            jax.ShapeDtypeStruct((R, D), F32),
            jax.ShapeDtypeStruct((R, D), F32),
        ),
        in_specs=[pl.BlockSpec(memory_space=pltpu.SMEM)] + [far] * 5,
        out_specs=(anywhere, whole, whole),
        scratch_shapes=[block] * 3
        + [pltpu.VMEM((1, D), BF), pltpu.VMEM((R, D), BF), pltpu.VMEM((R, D), BF)]
        + [pieces] * (3 * C)
        + [pltpu.VMEM((R, D), BF), tiles, tiles, tile, tiles]
        + [tile] * 4
        + [pltpu.VMEM((NY, 2 * R, W), BF)] * 2
        + [pltpu.VMEM((2 * NZ, R, 128), BF), pltpu.VMEM((NZ, 2, R, 128), BF), pltpu.VMEM((2 * NZ, R, 128), BF)]
        + [pltpu.VMEM((NY, TILES, R, 128), BF)] * 2
        + [dma((10,)), dma((10,)), dma((C + 4,)), dma((WINDOW,)), dma((C,)), dma((C,))],
        compiler_params=pltpu.CompilerParams(collective_id=0, has_side_effects=True, vmem_limit_bytes=40 << 20),
        name="adapter_step",
    )(wiring, *(pltpu.with_memory_space_constraint(v, pltpu.HBM) for v in operands))
    fwd, down_sum, up_sum = pl.pallas_call(
        copy_out,
        out_shape=tuple(jax.ShapeDtypeStruct(v.shape, v.dtype) for v in results),
        in_specs=[anywhere] * 3,
        out_specs=(anywhere,) * 3,
        scratch_shapes=[dma((3,))],
        name="copy_out",
    )(*(pltpu.with_memory_space_constraint(v, pltpu.VMEM) for v in results))
    return fwd[None], down_sum.T[None], up_sum[None]


def solution(mesh):
    in_specs = (
        P("section", "peer", None),
        P("section", "peer", None),
        P("section", None),
        P("section", None, None),
        P("section", None, None),
        P("section", "peer"),
    )
    out_specs = (P("section", "peer", None), P("section", None, None), P("section", None, None))
    return jax.shard_map(shards, mesh=mesh, in_specs=in_specs, out_specs=out_specs, check_vma=False)
```
